512 devices in a mesh: lon: 64 (over z, y_hi, core), ch: 8 (over x, y_lo).
Axes of the slice: x: 4, y: 8 (y_hi: 4, y_lo: 2; y = y_hi * 2 + y_lo), z: 8, core: 2. Of those that a mesh axis runs over, the one named last changes fastest.
Arguments:
- features: bfloat16 [512, 1, 8, 8192], P('ch', None, None, 'lon'), may hold values from -160 to 160, as said below
- group_norm_gain: float32 [512], P('ch'), may hold values from 0.5 to 2
- group_norm_bias: float32 [512], P('ch'), may hold values from -1 to 1
- kernel: bfloat16 [3, 3, 512, 512], P(None, None, 'ch'), may hold values from -0.058925565 to 0.058925565, as said below
- cotangent: bfloat16 [512, 1, 8, 8192], P('ch', None, None, 'lon'), may hold values from -10 to 10, as said below
Outputs:
- conv_out: bfloat16 [512, 1, 8, 8192], P('ch', None, None, 'lon')
- feature_map_gradient: bfloat16 [512, 1, 8, 8192], P('ch', None, None, 'lon')
- kernel_grad: float32 [3, 3, 512, 512], P(None, None, 'ch')
The draws below stay inside these ranges and needn't reach their ends.
Inputs may be any that keep to these rules, and one draw needn't show every extreme that they name: `features`: Real-valued feature map whose magnitude varies between rows and between longitudes, with a per-channel offset. `kernel`: Real-valued weights of standard deviation about (4608)^(-1/2). `cotangent`: Real-valued output gradient.
All inputs are finite; a program needn't handle non-finite values.
Results may differ from the reference program's by a relative error of at most 0.005.
Values may be sent and summed in bfloat16 or wider, within the bound.
A program may use at most 64 MiB of HBM per device.

```python
import math
import jax
import jax.numpy as jnp
from jax import lax

C = 512
O = 512
G = 32
F = 1
H = 8
W = 8192


def feature_parts(key):
    keys = jax.random.split(jax.random.fold_in(key, 7), 4)
    along = jnp.arange(W, dtype=jnp.float32) / W
    col_scale = jnp.exp(math.log(3.0) * along + jax.random.uniform(keys[0], (W,), jnp.float32, 0.0, math.log(3.4)))
    row_scale = jnp.exp(jax.random.uniform(keys[1], (H,), jnp.float32, 0.0, math.log(3.0)))
    offsets = 0.5 * jax.random.normal(keys[2], (C,), jnp.float32)
    base = jnp.clip(jax.random.normal(keys[3], (C, F, H, W), jnp.float32), -4.0, 4.0)
    field = base * row_scale[None, None, :, None] * col_scale[None, None, None, :] + offsets[:, None, None, None]
    return (base, field)


def shared_kernel(key):
    raw = jax.random.normal(jax.random.fold_in(key, 13), (3, 3, C, O), jnp.float32)
    return jnp.clip(raw, -4.0, 4.0) * (9.0 * C) ** (-0.5)


def draw_features(key, part):
    base, field = feature_parts(key)
    return field.astype(jnp.bfloat16)


def draw_kernel(key, part):
    return shared_kernel(key).astype(jnp.bfloat16)


def draw_cotangent(key, part):
    keys = jax.random.split(jax.random.fold_in(key, 11), 2)
    base, field = feature_parts(key)
    center = shared_kernel(key)[1, 1].astype(jnp.bfloat16).astype(jnp.float32)
    mixed = jnp.einsum('co,cfhw->ofhw', center, base, precision=lax.Precision.HIGHEST)
    noise = jnp.clip(jax.random.normal(keys[0], (O, F, H, W), jnp.float32), -4.0, 4.0)
    strength = 2.0
    offsets = 0.05 * jax.random.normal(keys[1], (O,), jnp.float32)
    values = jnp.clip(strength * mixed + noise + offsets[:, None, None, None], -10.0, 10.0)
    return values.astype(jnp.bfloat16)


def shard_levels(stream_key, shape, pieces, smallest, high):
    level, own = 1.0, jax.random.fold_in(stream_key, 6)
    for position, parts in pieces:
        steps = jnp.exp(jax.random.uniform(jax.random.fold_in(own, position), (parts,), jnp.float32, smallest / len(pieces), high / len(pieces)))
        level = level * jnp.repeat(steps, shape[position] // parts).reshape([-1 if axis == position else 1 for axis in range(len(shape))])
    return level


def setup_inputs(seed: int = 0) -> dict:
    streams_of = jax.random.split(jax.random.key(seed), 6)
    features = draw_features(jax.random.fold_in(streams_of[5], 71), 0)
    group_norm_gain = jnp.clip(jnp.exp(math.log(2.0) - 1.3862944 * jax.random.uniform(streams_of[1], (C,), jnp.float32) ** shard_levels(streams_of[1], (C,), ((0, 8),), -0.2, 0.2)), 0.5, 2.0)
    group_norm_bias = jnp.clip(jax.random.uniform(streams_of[2], (C,), jnp.float32, -1.0, 1.0) * shard_levels(streams_of[2], (C,), ((0, 8),), -0.4, 0.0), -1.0, 1.0)
    kernel = draw_kernel(jax.random.fold_in(streams_of[5], 71), 0)
    cotangent = draw_cotangent(jax.random.fold_in(streams_of[5], 71), 0)
    return dict(features=features, group_norm_gain=group_norm_gain, group_norm_bias=group_norm_bias, kernel=kernel, cotangent=cotangent)


def shifted(field, row_off, col_off):
    height = field.shape[2]
    padded = jnp.pad(field, ((0, 0), (0, 0), (1, 1), (0, 0)))
    rows = padded[:, :, row_off:row_off + height, :]
    return jnp.roll(rows, 1 - col_off, axis=3)

def group_totals(field):
    return field.reshape(G, -1).sum(axis=1)

def channel_values(values):
    return jnp.repeat(values, C // G)[:, None, None, None]

def reference(features, group_norm_gain, group_norm_bias, kernel, cotangent):
    feature_map = features.astype(jnp.float32)
    element_count = float(C // G * F * H * W)
    group_mean = group_totals(feature_map) / element_count
    var = group_totals(feature_map * feature_map) / element_count - group_mean * group_mean
    inverse_deviation = 1.0 / jnp.sqrt(var + 1e-06)
    normalized_input = (feature_map - channel_values(group_mean)) * channel_values(inverse_deviation)
    preactivation = normalized_input * group_norm_gain[:, None, None, None] + group_norm_bias[:, None, None, None]
    sig = jax.nn.sigmoid(preactivation)
    act = (preactivation * sig).astype(jnp.bfloat16)
    act_f = act.astype(jnp.float32)
    kern_f = kernel.astype(jnp.float32)
    grad_f = cotangent.astype(jnp.float32)
    conv_out = jnp.zeros((O, F, H, W), jnp.float32)
    act_grad = jnp.zeros((C, F, H, W), jnp.float32)
    grad_rows = []
    for row_off in range(3):
        grad_cols = []
        for col_off in range(3):
            moved = shifted(act_f, row_off, col_off)
            conv_out = conv_out + jnp.einsum('co,cfhw->ofhw', kern_f[row_off, col_off], moved)
            grad_cols.append(jnp.einsum('cfhw,ofhw->co', moved, grad_f))
            back = shifted(grad_f, 2 - row_off, 2 - col_off)
            act_grad = act_grad + jnp.einsum('co,ofhw->cfhw', kern_f[row_off, col_off], back)
        grad_rows.append(jnp.stack(grad_cols))
    kernel_grad = jnp.stack(grad_rows) * float(F * H * W) ** (-0.5)
    preactivation_gradient = act_grad * sig * (1.0 + preactivation * (1.0 - sig))
    normalized_input_gradient = preactivation_gradient * group_norm_gain[:, None, None, None]
    linear_sum = group_totals(normalized_input_gradient)
    quadratic_sum = group_totals(normalized_input_gradient * normalized_input)
    feature_map_gradient = channel_values(inverse_deviation) * (normalized_input_gradient - channel_values(linear_sum) / element_count - normalized_input * channel_values(quadratic_sum) / element_count)
    return (conv_out.astype(jnp.bfloat16), feature_map_gradient.astype(jnp.bfloat16), kernel_grad)
```

```python
import functools

import jax
import jax.numpy as jnp
from jax import lax
from jax.experimental import pallas as pl
from jax.experimental.pallas import tpu as pltpu
from jax.sharding import PartitionSpec as P

C = 512
G = 32
CL = 64
H = 8
W = 128
S = H * W
NZ, NY = 8, 4
OWN_Z = 6
NQ = OWN_Z * NY
CH = 48
MESH = pl.DeviceIdType.MESH
F32 = jnp.float32
BF16 = jnp.bfloat16


def body(
    feat, gain, bias, w, cot,
    conv_out, fgrad, kgrad,
    tmp, x2, xh, dact, patch, wt, cotall, halo, edge, edge_in,
    y_st, z_st, y_t, z_t, convb, convr, g3, gsend, gcore, hb, rsbuf, gfin, zz, agr,
    edge_s, edge_r, cot_s, cot_r, halo_s, halo_r,
    yst_s, yst_r, zst_s, zst_r, yt_s, yt_r, zt_s, zt_r,
    conv_s, conv_r, core_s, core_r, rs_s, rs_r, ag_s, ag_r, fw_s, fw_r,
):
    lon = lax.axis_index("lon")
    ch = lax.axis_index("ch")
    z, yc = lon // 8, lon % 8
    yh, core = yc // 2, yc % 2
    n_lon = 64

    def at_lon(d):
        return (lax.rem(lon + d + n_lon, n_lon), ch)

    def at_ch(k):
        return (lon, lax.rem(ch + k, 8))

    def at_yc(k):
        return (z * 8 + lax.rem(yc + k, 8), ch)

    def at_z(k):
        return (lax.rem(z + k, 8) * 8 + yc, ch)

    partner = (lon + 1 - 2 * core, ch)

    def remote(src, dst, ss, rs, dev):
        return pltpu.make_async_remote_copy(
            src_ref=src, dst_ref=dst, send_sem=ss, recv_sem=rs, device_id=dev, device_id_type=MESH
        )

    barrier = pltpu.get_barrier_semaphore()
    for k in range(1, 8):
        for where in (at_ch, at_yc, at_z):
            pl.semaphore_signal(barrier, inc=1, device_id=where(k), device_id_type=MESH)
    for d in (-1, 1):
        pl.semaphore_signal(barrier, inc=1, device_id=at_lon(d), device_id_type=MESH)

    lane = lax.broadcasted_iota(jnp.int32, (CL, W), 1)
    group = lax.broadcasted_iota(jnp.int32, (CL, W), 0) // 16

    my_rows = pl.ds(pl.multiple_of(ch * CL, CL), CL)

    tmp[...] = cot[...].astype(F32)
    e = jnp.zeros((CL, W), F32)
    for h in range(H):
        row = tmp[pl.ds(h, CL, stride=H), :]
        cotall[my_rows, h * W:(h + 1) * W] = row.astype(BF16)
        e = jnp.where(lane == h, row[:, W - 1:W], e)
        e = jnp.where(lane == H + h, row[:, 0:1], e)
    edge[0:CL, :] = e.astype(BF16)
    tmp[...] = feat[...].astype(F32)
    e = jnp.zeros((CL, W), F32)
    total = jnp.zeros((CL, W), F32)
    total2 = jnp.zeros((CL, W), F32)
    for h in range(H):
        row = tmp[pl.ds(h, CL, stride=H), :]
        x2[:, h * W:(h + 1) * W] = row
        total += row
        total2 += row * row
        e = jnp.where(lane == h, row[:, W - 1:W], e)
        e = jnp.where(lane == H + h, row[:, 0:1], e)
    edge[CL:2 * CL, :] = e.astype(BF16)

    def pack(a, b):
        a = jnp.sum(a, axis=1, keepdims=True)
        b = jnp.sum(b, axis=1, keepdims=True)
        both = jnp.where(lane == group, a, 0.0) + jnp.where(lane == group + 4, b, 0.0)
        return jnp.sum(both, axis=0, keepdims=True)

    def unpack(vec):
        full = jnp.broadcast_to(vec, (CL, W))
        a = jnp.sum(jnp.where(lane == group, full, 0.0), axis=1, keepdims=True)
        b = jnp.sum(jnp.where(lane == group + 4, full, 0.0), axis=1, keepdims=True)
        return a, b

    def column(ref):
        r = lax.broadcasted_iota(jnp.int32, (CL, CL), 0)
        c = lax.broadcasted_iota(jnp.int32, (CL, CL), 1)
        return jnp.sum(jnp.where(r == c, jnp.broadcast_to(ref[...], (CL, CL)), 0.0), axis=1, keepdims=True)

    def peers_copy(buf, ss, rs, where):
        return [remote(buf.at[0], buf.at[k], ss.at[k], rs.at[k], where(k)) for k in range(1, 8)]

    def add_up(buf):
        acc = buf[0]
        for k in range(1, 8):
            acc = acc + buf[k]
        return acc

    y_st[0] = pack(total, total2)
    pl.semaphore_wait(barrier, 23)

    yst = peers_copy(y_st, yst_s, yst_r, at_yc)
    for cp in yst:
        cp.start()
    edges = [
        remote(edge, edge_in.at[0], edge_s.at[0], edge_r.at[0], at_lon(1)),
        remote(edge, edge_in.at[1], edge_s.at[1], edge_r.at[1], at_lon(-1)),
    ]
    for cp in edges:
        cp.start()
    cots = [
        remote(cotall.at[my_rows], cotall.at[my_rows], cot_s.at[k], cot_r.at[k], at_ch(k))
        for k in (4, 3, 5, 2, 6, 7, 1)
    ]
    for cp in cots:
        cp.start()

    for i in range(4):
        wt[:, i * 128:(i + 1) * 128] = w[i * 128:(i + 1) * 128, :].astype(F32).T.astype(BF16)
    wt[:, 512:576] = w[512:576, :].astype(F32).T.astype(BF16)

    for cp in yst:
        cp.wait_recv()
    z_st[0] = add_up(y_st)
    zst = peers_copy(z_st, zst_s, zst_r, at_z)
    for cp in zst:
        cp.start()

    for cp in edges:
        cp.wait_recv()
    lane2 = lax.broadcasted_iota(jnp.int32, (2 * CL, W), 1)
    rim = jnp.where(lane2 < H, edge_in[0].astype(F32), edge_in[1].astype(F32))
    halo[my_rows, :] = rim[0:CL].astype(BF16)
    halos = [
        remote(halo.at[my_rows], halo.at[my_rows], halo_s.at[k], halo_r.at[k], at_ch(k))
        for k in range(1, 8)
    ]
    for cp in halos:
        cp.start()

    gain_c = column(gain)
    bias_c = column(bias)
    n = float(16 * H * W * n_lon)
    zero = jnp.zeros((192, W), BF16)
    patch[0:192, 0:W] = zero
    patch[384:576, S - W:S] = zero

    for cp in zst:
        cp.wait_recv()
    m1, m2 = unpack(add_up(z_st))
    mean = m1 / n
    var = m2 / n - mean * mean
    rstd = 1.0 / jnp.sqrt(var + 1e-06)

    rim_pre = (rim[CL:2 * CL] - mean) * rstd * gain_c + bias_c
    rim_act = rim_pre * jax.nn.sigmoid(rim_pre)
    for h in range(H):
        cols = slice(h * W, (h + 1) * W)
        norm = (x2[:, cols] - mean) * rstd
        pre = norm * gain_c + bias_c
        sig = jax.nn.sigmoid(pre)
        xh[:, cols] = norm
        dact[:, cols] = sig * (1.0 + pre * (1.0 - sig)) * gain_c
        act = pre * sig
        left = jnp.where(lane == 0, rim_act[:, h:h + 1], pltpu.roll(act, 1, 1))
        right = jnp.where(lane == W - 1, rim_act[:, H + h:H + h + 1], pltpu.roll(act, W - 1, 1))
        for s, v in enumerate((left, act, right)):
            v = v.astype(BF16)
            for r in range(3):
                to = h + 1 - r
                if 0 <= to < H:
                    patch[r * 192 + s * CL:r * 192 + (s + 1) * CL, to * W:(to + 1) * W] = v

    for cp in cots:
        cp.wait_recv()

    def kg_step(i, _):
        rows = pl.ds(pl.multiple_of(i * 256, 256), 256)
        part = lax.dot_general(
            patch[...], cotall[rows, :], (((1,), (1,)), ((), ())), preferred_element_type=F32
        )
        for rc in range(12):
            for c in range(2):
                g3[rc // 6, (rc % 6) * 4 + 2 * i + c] = part[rc * CH:(rc + 1) * CH, c * W:(c + 1) * W]
        return 0

    lax.fori_loop(0, 2, kg_step, 0)
    gsend[...] = g3[1 - core].astype(BF16)
    swap = remote(gsend, gcore, core_s.at[0], core_r.at[0], partner)
    swap.start()

    def conv_step(i, _):
        cols = pl.ds(pl.multiple_of(i * 256, 256), 256)
        convb[:, cols] = jnp.dot(wt[...], patch[:, cols], preferred_element_type=F32).astype(BF16)
        return 0

    swap.wait_recv()
    hb[...] = (g3[core] + gcore[...].astype(F32)).astype(BF16)

    def target(k):
        tz, ty = lax.rem(z + k // NY, NZ), lax.rem(yh + k % NY, NY)
        return tz, ty, (tz * 8 + ty * 2 + core, ch)

    my_q = z * NY + yh
    owner = z < OWN_Z

    def rs_copy(k):
        tz, ty, dev = target(k)
        return tz, remote(hb.at[lax.min(tz, OWN_Z - 1) * NY + ty], rsbuf.at[k], rs_s.at[k], rs_r.at[k], dev)

    def rs_send(k, _):
        tz, cp = rs_copy(k)

        @pl.when(tz < OWN_Z)
        def _():
            cp.start()

        return 0

    lax.fori_loop(1, 32, rs_send, 0)

    lax.fori_loop(0, 4, conv_step, 0)

    def ch_rows(k):
        return pl.ds(pl.multiple_of(lax.rem(ch + k, 8) * CL, CL), CL)

    convs = [
        remote(convb.at[ch_rows(k)], convr.at[k], conv_s.at[k], conv_r.at[k], at_ch(k))
        for k in (4, 3, 5, 2, 6, 7, 1)
    ]
    for cp in convs:
        cp.start()

    for cp in halos:
        cp.wait_recv()

    def z_step(i, _):
        cols = pl.ds(pl.multiple_of(i * 256, 256), 256)
        zz[:, cols] = jnp.dot(w[...], cotall[:, cols], preferred_element_type=F32)
        return 0

    lax.fori_loop(0, 4, z_step, 0)
    zh = jnp.dot(w[...], halo[...], preferred_element_type=F32)

    def zrows(r, s):
        return slice(r * 192 + s * CL, r * 192 + (s + 1) * CL)

    def rim_sum(s):
        up = jnp.where((lane % H) < H - 1, pltpu.roll(zh[zrows(0, s)], W - 1, 1), 0.0)
        down = jnp.where((lane % H) > 0, pltpu.roll(zh[zrows(2, s)], 1, 1), 0.0)
        return up + zh[zrows(1, s)] + down

    rim0, rim2 = rim_sum(0), rim_sum(2)
    t1 = jnp.zeros((CL, W), F32)
    t2 = jnp.zeros((CL, W), F32)
    for h in range(H):
        u = []
        for s in range(3):
            acc = zz[zrows(1, s), h * W:(h + 1) * W]
            if h + 1 < H:
                acc = acc + zz[zrows(0, s), (h + 1) * W:(h + 2) * W]
            if h >= 1:
                acc = acc + zz[zrows(2, s), (h - 1) * W:h * W]
            u.append(acc)
        agrad = u[1]
        agrad = agrad + jnp.where(lane == W - 1, rim0[:, H + h:H + h + 1], pltpu.roll(u[0], W - 1, 1))
        agrad = agrad + jnp.where(lane == 0, rim2[:, h:h + 1], pltpu.roll(u[2], 1, 1))
        cols = slice(h * W, (h + 1) * W)
        ng = agrad * dact[:, cols]
        agr[:, cols] = ng
        t1 += ng
        t2 += ng * xh[:, cols]
    y_t[0] = pack(t1, t2)
    yt = peers_copy(y_t, yt_s, yt_r, at_yc)
    for cp in yt:
        cp.start()

    def ag_copy(k):
        _, _, dev = target(k)
        q = lax.min(z, OWN_Z - 1) * NY + yh
        return remote(gfin.at[core, q], gfin.at[core, q], ag_s.at[k], ag_r.at[q], dev)

    @pl.when(owner)
    def _():
        def take(k, acc):
            rs_copy(k)[1].wait_recv()
            return acc + rsbuf[k].astype(F32)

        acc = lax.fori_loop(1, 32, take, hb[my_q].astype(F32))
        gfin[core, my_q] = acc.astype(BF16)

        def give(k, _):
            ag_copy(k).start()
            return 0

        lax.fori_loop(1, 32, give, 0)

    for cp in yt:
        cp.wait_recv()
    z_t[0] = add_up(y_t)
    zt = peers_copy(z_t, zt_s, zt_r, at_z)
    for cp in zt:
        cp.start()

    for cp in convs:
        cp.wait_recv()
    for h in range(H):
        cols = slice(h * W, (h + 1) * W)
        acc = convb[my_rows, cols].astype(F32)
        for k in range(1, 8):
            acc = acc + convr[k, :, cols].astype(F32)
        conv_out[pl.ds(h, CL, stride=H), :] = acc

    for cp in zt:
        cp.wait_recv()
    q1, q2 = unpack(add_up(z_t))
    q1 = q1 / n
    q2 = q2 / n
    for h in range(H):
        cols = slice(h * W, (h + 1) * W)
        fgrad[pl.ds(h, CL, stride=H), :] = rstd * (agr[:, cols] - q1 - xh[:, cols] * q2)

    def forward(q, half):
        return remote(gfin.at[half, q], gfin.at[half, q], fw_s.at[q], fw_r.at[q], partner)

    def relay(q, _):
        @pl.when(q != my_q)
        def _():
            remote(gfin.at[core, q], gfin.at[core, q], ag_s.at[0], ag_r.at[q], partner).wait_recv()

        forward(q, core).start()
        return 0

    lax.fori_loop(0, NQ, relay, 0)

    def relayed(q, _):
        forward(q, 1 - core).wait_recv()
        return 0

    lax.fori_loop(0, NQ, relayed, 0)
    for half in range(2):
        for rc in range(6):
            for c in range(4):
                top = (half * 6 + rc) * CH
                kgrad[top:top + CH, c * W:(c + 1) * W] = gfin[half, rc * 4 + c]

    for cp in yst + edges + cots + zst + halos + [swap] + convs + yt + zt:
        cp.wait_send()

    def rs_done(k, _):
        tz, cp = rs_copy(k)

        @pl.when(tz < OWN_Z)
        def _():
            cp.wait_send()

        return 0

    lax.fori_loop(1, 32, rs_done, 0)

    @pl.when(owner)
    def _():
        def given(k, _):
            ag_copy(k).wait_send()
            return 0

        lax.fori_loop(1, 32, given, 0)

    def fw_done(q, _):
        forward(q, core).wait_send()
        return 0

    lax.fori_loop(0, NQ, fw_done, 0)


def per_device(features, gain, bias, kernel, cotangent):
    vmem = pl.BlockSpec(memory_space=pltpu.VMEM)
    dma = pltpu.SemaphoreType.DMA
    conv_out, fgrad, kgrad = pl.pallas_call(
        body,
        out_shape=(
            jax.ShapeDtypeStruct((CL * H, W), F32),
            jax.ShapeDtypeStruct((CL * H, W), F32),
            jax.ShapeDtypeStruct((9 * CL, C), BF16),
        ),
        in_specs=[vmem] * 5,
        out_specs=(vmem,) * 3,
        scratch_shapes=[
            pltpu.VMEM((CL * H, W), F32),
            pltpu.VMEM((CL, S), F32),
            pltpu.VMEM((CL, S), F32),
            pltpu.VMEM((CL, S), F32),
            pltpu.VMEM((9 * CL, S), BF16),
            pltpu.VMEM((C, 9 * CL), BF16),
            pltpu.VMEM((C, S), BF16),
            pltpu.VMEM((C, W), BF16),
            pltpu.VMEM((2 * CL, W), BF16),
            pltpu.VMEM((2, 2 * CL, W), BF16),
            pltpu.VMEM((8, 1, W), F32),
            pltpu.VMEM((8, 1, W), F32),
            pltpu.VMEM((8, 1, W), F32),
            pltpu.VMEM((8, 1, W), F32),
            pltpu.VMEM((C, S), BF16),
            pltpu.VMEM((8, CL, S), BF16),
            pltpu.VMEM((2, NQ, CH, W), F32),
            pltpu.VMEM((NQ, CH, W), BF16),
            pltpu.VMEM((NQ, CH, W), BF16),
            pltpu.VMEM((NQ, CH, W), BF16),
            pltpu.VMEM((32, CH, W), BF16),
            pltpu.VMEM((2, NQ, CH, W), BF16),
            pltpu.VMEM((9 * CL, S), F32),
            pltpu.VMEM((CL, S), F32),
            dma((2,)), dma((2,)),
            dma((8,)), dma((8,)),
            dma((8,)), dma((8,)),
            dma((8,)), dma((8,)),
            dma((8,)), dma((8,)),
            dma((8,)), dma((8,)),
            dma((8,)), dma((8,)),
            dma((8,)), dma((8,)),
            dma((1,)), dma((1,)),
            dma((32,)), dma((32,)),
            dma((32,)), dma((NQ,)),
            dma((NQ,)), dma((NQ,)),
        ],
        compiler_params=pltpu.CompilerParams(
            collective_id=0, has_side_effects=True, vmem_limit_bytes=40 * 1024 * 1024
        ),
        name="strip",
    )(
        features.reshape(CL * H, W),
        gain.reshape(1, CL),
        bias.reshape(1, CL),
        kernel.reshape(9 * CL, C),
        cotangent.reshape(CL * H, W),
    )
    shape = features.shape
    return (
        conv_out.astype(BF16).reshape(shape),
        fgrad.astype(BF16).reshape(shape),
        (kgrad.astype(F32) * (2.0 ** -8)).reshape(kernel.shape),
    )


def solution(mesh):
    in_specs = (
        P("ch", None, None, "lon"),
        P("ch"),
        P("ch"),
        P(None, None, "ch", None),
        P("ch", None, None, "lon"),
    )
    out_specs = (P("ch", None, None, "lon"), P("ch", None, None, "lon"), P(None, None, "ch", None))
    return jax.shard_map(
        per_device, mesh=mesh, in_specs=in_specs, out_specs=out_specs, check_vma=False
    )
```

```python
import functools

import jax
import jax.numpy as jnp
from jax import lax
from jax.experimental import pallas as pl
from jax.experimental.pallas import tpu as pltpu
from jax.sharding import PartitionSpec as P

C = 512
G = 32
CL = 64
H = 8
W = 128
S = H * W
NZ, NY = 8, 4
NQ = 24
CH = 48
FAR = sorted(
    ((dz, dy) for dz in range(NZ) for dy in range(NY) if dz or dy),
    key=lambda o: -(min(o[0], NZ - o[0]) + 2 * min(o[1], NY - o[1])),
)
MESH = pl.DeviceIdType.MESH
F32 = jnp.float32
BF16 = jnp.bfloat16


def body(
    feat_in, gain, bias, w_in, cot_in,
    conv_out, fgrad, kgrad,
    feat, cot, w, in_s, tmp, x2, xh, dact, patch, wt, cotall, halo, edge, edge_in,
    c_st, y_st, z_st, c_t, y_t, z_t,
    convb, convr, convp, convq, g3, gsend, gcore, hb, rsbuf, gfin, zz, agr, conv_f, fg_f,
    edge_s, edge_r, cot_s, cot_r, halo_s, halo_r, st_s, st_r, t_s, t_r,
    conv_s, conv_r, core_s, core_r, rs_s, rs_r, ag_s, ag_r, fw_s, fw_r, kg_s, out_s,
):
    lon = lax.axis_index("lon")
    ch = lax.axis_index("ch")
    z, yc = lon // 8, lon % 8
    yh, core = yc // 2, yc % 2
    x, yl = ch // 2, ch % 2
    n_lon = 64

    def at_lon(d):
        return (lax.rem(lon + d + n_lon, n_lon), ch)

    def at_ch(k):
        return (lon, lax.rem(ch + k, 8))

    def at_x(k):
        return (lon, lax.rem(x + k, 4) * 2 + yl)

    def at_y(k):
        return (z * 8 + lax.rem(yh + k, NY) * 2 + core, ch)

    def at_z(k):
        return (lax.rem(z + k, 8) * 8 + yc, ch)

    partner = (lon + 1 - 2 * core, ch)
    beside = (lon, ch + 1 - 2 * yl)

    def remote(src, dst, ss, rs, dev):
        return pltpu.make_async_remote_copy(
            src_ref=src, dst_ref=dst, send_sem=ss, recv_sem=rs, device_id=dev, device_id_type=MESH
        )

    loads = [
        pltpu.make_async_copy(a, b, in_s.at[i])
        for i, (a, b) in enumerate(((cot_in, cot), (feat_in, feat), (w_in, w)))
    ]
    for cp in loads:
        cp.start()

    barrier = pltpu.get_barrier_semaphore()
    for count, where in ((8, at_ch), (8, at_z), (NY, at_y)):
        for k in range(1, count):
            pl.semaphore_signal(barrier, inc=1, device_id=where(k), device_id_type=MESH)
    for d in (-1, 1):
        pl.semaphore_signal(barrier, inc=1, device_id=at_lon(d), device_id_type=MESH)

    lane = lax.broadcasted_iota(jnp.int32, (CL, W), 1)
    group = lax.broadcasted_iota(jnp.int32, (CL, W), 0) // 16

    my_rows = pl.ds(pl.multiple_of(ch * CL, CL), CL)

    loads[0].wait()
    tmp[...] = cot[...].astype(F32)
    e = jnp.zeros((CL, W), F32)
    for h in range(H):
        row = tmp[pl.ds(h, CL, stride=H), :]
        cotall[my_rows, h * W:(h + 1) * W] = row.astype(BF16)
        e = jnp.where(lane == h, row[:, W - 1:W], e)
        e = jnp.where(lane == H + h, row[:, 0:1], e)
    edge[0:CL, :] = e.astype(BF16)
    loads[1].wait()
    tmp[...] = feat[...].astype(F32)
    e = jnp.zeros((CL, W), F32)
    total = jnp.zeros((CL, W), F32)
    total2 = jnp.zeros((CL, W), F32)
    for h in range(H):
        row = tmp[pl.ds(h, CL, stride=H), :]
        x2[:, h * W:(h + 1) * W] = row
        total += row
        total2 += row * row
        e = jnp.where(lane == h, row[:, W - 1:W], e)
        e = jnp.where(lane == H + h, row[:, 0:1], e)
    edge[CL:2 * CL, :] = e.astype(BF16)

    def pack(a, b):
        a = jnp.sum(a, axis=1, keepdims=True)
        b = jnp.sum(b, axis=1, keepdims=True)
        both = jnp.where(lane == group, a, 0.0) + jnp.where(lane == group + 4, b, 0.0)
        return jnp.sum(both, axis=0, keepdims=True)

    def unpack(vec):
        full = jnp.broadcast_to(vec, (CL, W))
        a = jnp.sum(jnp.where(lane == group, full, 0.0), axis=1, keepdims=True)
        b = jnp.sum(jnp.where(lane == group + 4, full, 0.0), axis=1, keepdims=True)
        return a, b

    def column(ref):
        r = lax.broadcasted_iota(jnp.int32, (CL, CL), 0)
        c = lax.broadcasted_iota(jnp.int32, (CL, CL), 1)
        return jnp.sum(jnp.where(r == c, jnp.broadcast_to(ref[...], (CL, CL)), 0.0), axis=1, keepdims=True)

    def rounds(bufs, ss, rs):
        def sends(buf, count, base, where):
            return [
                remote(buf.at[0], buf.at[k], ss.at[base + k], rs.at[base + k], where(k))
                for k in range(1, count)
            ]

        return (
            sends(bufs[0], 2, 0, lambda k: partner),
            sends(bufs[1], NY, 2, at_y),
            sends(bufs[2], NZ, 6, at_z),
        )

    def start(copies):
        for cp in copies:
            cp.start()

    def arrive(copies):
        for cp in copies:
            cp.wait_recv()

    def add_up(buf):
        acc = buf[0]
        for k in range(1, buf.shape[0]):
            acc = acc + buf[k]
        return acc

    c_st[0] = pack(total, total2)
    pl.semaphore_wait(barrier, 19)

    st = rounds((c_st, y_st, z_st), st_s, st_r)
    start(st[0])
    edges = [
        remote(edge, edge_in.at[0], edge_s.at[0], edge_r.at[0], at_lon(1)),
        remote(edge, edge_in.at[1], edge_s.at[1], edge_r.at[1], at_lon(-1)),
    ]
    start(edges)
    its_rows = pl.ds(pl.multiple_of((ch + 1 - 2 * yl) * CL, CL), CL)
    cot_pair = [remote(cotall.at[my_rows], cotall.at[my_rows], cot_s.at[0], cot_r.at[0], beside)]
    cot_mine = [
        remote(cotall.at[my_rows], cotall.at[my_rows], cot_s.at[k], cot_r.at[k], at_x(k))
        for k in (1, 3, 2)
    ]
    cot_its = [
        remote(cotall.at[its_rows], cotall.at[its_rows], cot_s.at[3 + k], cot_r.at[3 + k], at_x(k))
        for k in (1, 3, 2)
    ]
    start(cot_pair + cot_mine)
    arrive(st[0])
    y_st[0] = add_up(c_st)
    start(st[1])

    loads[2].wait()
    for i in range(4):
        wt[:, i * 128:(i + 1) * 128] = w[i * 128:(i + 1) * 128, :].astype(F32).T.astype(BF16)
    wt[:, 512:576] = w[512:576, :].astype(F32).T.astype(BF16)

    arrive(cot_pair)
    start(cot_its)
    arrive(st[1])
    z_st[0] = add_up(y_st)
    start(st[2])

    arrive(edges)
    lane2 = lax.broadcasted_iota(jnp.int32, (2 * CL, W), 1)
    rim = jnp.where(lane2 < H, edge_in[0].astype(F32), edge_in[1].astype(F32))
    halo[my_rows, :] = rim[0:CL].astype(BF16)
    halos = [
        remote(halo.at[my_rows], halo.at[my_rows], halo_s.at[k], halo_r.at[k], at_ch(k))
        for k in range(1, 8)
    ]
    start(halos)

    gain_c = column(gain)
    bias_c = column(bias)
    n = float(16 * H * W * n_lon)
    zero = jnp.zeros((192, W), BF16)
    patch[0:192, 0:W] = zero
    patch[384:576, S - W:S] = zero

    arrive(st[2])
    m1, m2 = unpack(add_up(z_st))
    mean = m1 / n
    var = m2 / n - mean * mean
    rstd = 1.0 / jnp.sqrt(var + 1e-06)

    rim_pre = (rim[CL:2 * CL] - mean) * rstd * gain_c + bias_c
    rim_act = rim_pre * jax.nn.sigmoid(rim_pre)
    for h in range(H):
        cols = slice(h * W, (h + 1) * W)
        norm = (x2[:, cols] - mean) * rstd
        pre = norm * gain_c + bias_c
        sig = jax.nn.sigmoid(pre)
        xh[:, cols] = norm
        dact[:, cols] = sig * (1.0 + pre * (1.0 - sig)) * gain_c
        act = pre * sig
        left = jnp.where(lane == 0, rim_act[:, h:h + 1], pltpu.roll(act, 1, 1))
        right = jnp.where(lane == W - 1, rim_act[:, H + h:H + h + 1], pltpu.roll(act, W - 1, 1))
        for s, v in enumerate((left, act, right)):
            v = v.astype(BF16)
            for r in range(3):
                to = h + 1 - r
                if 0 <= to < H:
                    patch[r * 192 + s * CL:r * 192 + (s + 1) * CL, to * W:(to + 1) * W] = v

    my_j = lax.rem(yh - z + 8, 4)
    my_q = my_j * NZ + z
    owner = my_j < 3

    def to(offset):
        tz, ty = lax.rem(z + offset[0], NZ), lax.rem(yh + offset[1], NY)
        j = lax.rem(ty - tz + 8, 4)
        return j < 3, lax.min(j, 2) * NZ + tz, (tz * 8 + ty * 2 + core, ch)

    def swap(i):
        return remote(gsend.at[i], gcore.at[i], core_s.at[i], core_r.at[i], partner)

    def rs_copy(i):
        takes, q, dev = to(FAR[i])
        return takes, q, remote(hb.at[q], rsbuf.at[i], rs_s.at[i], rs_r.at[i], dev)

    def send_sums(i):
        lc = lax.rem(x + (0, 1, 3, 2)[i], 4)
        swap(i).wait_recv()
        for rc in range(6):
            hb[lc * 6 + rc] = (g3[core, i, rc] + gcore[i, rc].astype(F32)).astype(BF16)
        for k in range(31):
            takes, q, cp = rs_copy(k)

            @pl.when(takes & (q >= lc * 6) & (q < lc * 6 + 6))
            def _(cp=cp):
                cp.start()

    for i in range(4):
        d = (0, 1, 3, 2)[i]
        if d:
            remote(cotall.at[my_rows], cotall.at[my_rows], cot_s.at[0], cot_r.at[4 - d], beside).wait_recv()
            remote(cotall.at[my_rows], cotall.at[my_rows], cot_s.at[0], cot_r.at[7 - d], beside).wait_recv()
        rows = pl.ds(pl.multiple_of(lax.rem(x + d, 4) * W, W), W)
        part = lax.dot_general(
            patch[...], cotall[rows, :], (((1,), (1,)), ((), ())), preferred_element_type=F32
        )
        for rc in range(12):
            g3[rc // 6, i, rc % 6] = part[rc * CH:(rc + 1) * CH]
        gsend[i] = g3[1 - core, i].astype(BF16)
        swap(i).start()
        if i:
            send_sums(i - 1)
    send_sums(3)

    def conv_step(i, _):
        cols = pl.ds(pl.multiple_of(i * 256, 256), 256)
        convb[:, cols] = jnp.dot(wt[...], patch[:, cols], preferred_element_type=F32).astype(BF16)
        return 0

    lax.fori_loop(0, 4, conv_step, 0)

    def pair_rows(k):
        return pl.ds(pl.multiple_of(lax.rem(x + k, 4) * W, W), W)

    convs = [
        remote(convb.at[pair_rows(k)], convr.at[k - 1], conv_s.at[k], conv_r.at[k], at_x(k))
        for k in (2, 1, 3)
    ]
    start(convs)

    arrive(halos)

    def z_step(i, _):
        cols = pl.ds(pl.multiple_of(i * 256, 256), 256)
        zz[:, cols] = jnp.dot(w[...], cotall[:, cols], preferred_element_type=F32)
        return 0

    lax.fori_loop(0, 4, z_step, 0)
    zh = jnp.dot(w[...], halo[...], preferred_element_type=F32)

    def zrows(r, s):
        return slice(r * 192 + s * CL, r * 192 + (s + 1) * CL)

    def rim_sum(s):
        up = jnp.where((lane % H) < H - 1, pltpu.roll(zh[zrows(0, s)], W - 1, 1), 0.0)
        down = jnp.where((lane % H) > 0, pltpu.roll(zh[zrows(2, s)], 1, 1), 0.0)
        return up + zh[zrows(1, s)] + down

    rim0, rim2 = rim_sum(0), rim_sum(2)
    t1 = jnp.zeros((CL, W), F32)
    t2 = jnp.zeros((CL, W), F32)
    for h in range(H):
        u = []
        for s in range(3):
            acc = zz[zrows(1, s), h * W:(h + 1) * W]
            if h + 1 < H:
                acc = acc + zz[zrows(0, s), (h + 1) * W:(h + 2) * W]
            if h >= 1:
                acc = acc + zz[zrows(2, s), (h - 1) * W:h * W]
            u.append(acc)
        agrad = u[1]
        agrad = agrad + jnp.where(lane == W - 1, rim0[:, H + h:H + h + 1], pltpu.roll(u[0], W - 1, 1))
        agrad = agrad + jnp.where(lane == 0, rim2[:, h:h + 1], pltpu.roll(u[2], 1, 1))
        cols = slice(h * W, (h + 1) * W)
        ng = agrad * dact[:, cols]
        agr[:, cols] = ng
        t1 += ng
        t2 += ng * xh[:, cols]
    c_t[0] = pack(t1, t2)
    tt = rounds((c_t, y_t, z_t), t_s, t_r)
    start(tt[0])
    arrive(tt[0])
    y_t[0] = add_up(c_t)
    start(tt[1])

    def ag_copy(k):
        q = lax.min(my_j, 2) * NZ + z
        return remote(gfin.at[core, q], gfin.at[core, q], ag_s.at[k], ag_r.at[q], to(FAR[k])[2])

    @pl.when(owner)
    def _():
        acc = hb[my_q].astype(F32)
        for k in reversed(range(31)):
            rs_copy(k)[2].wait_recv()
            acc = acc + rsbuf[k].astype(F32)
        gfin[core, my_q] = acc.astype(BF16)
        for k in range(31):
            ag_copy(k).start()

    arrive(tt[1])
    z_t[0] = add_up(y_t)
    start(tt[2])

    arrive(convs)
    for half in range(2):
        for h in range(H):
            cols = slice(h * W, (h + 1) * W)
            top = pl.ds(pl.multiple_of(x * W + half * CL, CL), CL)
            acc = convb[top, cols].astype(F32)
            for k in range(3):
                acc = acc + convr[k, half * CL:(half + 1) * CL, cols].astype(F32)
            convp[half, :, cols] = acc.astype(BF16)
    conv_pair = remote(convp.at[1 - yl], convq, conv_s.at[0], conv_r.at[0], beside)
    conv_pair.start()

    arrive(tt[2])
    q1, q2 = unpack(add_up(z_t))
    q1 = q1 / n
    q2 = q2 / n
    for h in range(H):
        cols = slice(h * W, (h + 1) * W)
        fg_f[pl.ds(h, CL, stride=H), :] = rstd * (agr[:, cols] - q1 - xh[:, cols] * q2)

    outs = [
        pltpu.make_async_copy(fg_f, fgrad, out_s.at[0]),
        pltpu.make_async_copy(conv_f, conv_out, out_s.at[1]),
    ]
    outs[0].start()

    arrive([conv_pair])
    for h in range(H):
        cols = slice(h * W, (h + 1) * W)
        conv_f[pl.ds(h, CL, stride=H), :] = convp[yl, :, cols].astype(F32) + convq[:, cols].astype(F32)
    outs[1].start()

    def forward(q, half):
        return remote(gfin.at[half, q], gfin.at[half, q], fw_s.at[q], fw_r.at[q], partner)

    def store(q, half):
        rows = pl.ds(pl.multiple_of((half * 6 + lax.rem(q, 6)) * CH, CH), CH)
        cols = pl.ds(pl.multiple_of(q // 6 * W, W), W)
        return pltpu.make_async_copy(gfin.at[half, q], kgrad.at[rows, cols], kg_s.at[half, q])

    def turn(i):
        return lax.rem(i + x * 6, NQ)

    def relay(i, _):
        q = turn(i)

        @pl.when(q != my_q)
        def _():
            remote(gfin.at[core, q], gfin.at[core, q], ag_s.at[0], ag_r.at[q], partner).wait_recv()

        forward(q, core).start()
        store(q, core).start()
        return 0

    lax.fori_loop(0, NQ, relay, 0)

    def relayed(i, _):
        q = turn(i)
        forward(q, 1 - core).wait_recv()
        store(q, 1 - core).start()
        return 0

    lax.fori_loop(0, NQ, relayed, 0)

    for cp in edges + cot_pair + cot_mine + cot_its + halos + convs + [conv_pair]:
        cp.wait_send()
    for part in st + tt:
        for cp in part:
            cp.wait_send()
    for i in range(4):
        swap(i).wait_send()
    for k in range(31):
        takes, _, cp = rs_copy(k)

        @pl.when(takes)
        def _(cp=cp):
            cp.wait_send()

    @pl.when(owner)
    def _():
        for k in range(31):
            ag_copy(k).wait_send()

    for cp in outs:
        cp.wait()

    def done(q, _):
        forward(q, core).wait_send()
        store(q, core).wait()
        store(q, 1 - core).wait()
        return 0

    lax.fori_loop(0, NQ, done, 0)


def per_device(features, gain, bias, kernel, cotangent):
    vmem = pl.BlockSpec(memory_space=pltpu.VMEM)
    hbm = pl.BlockSpec(memory_space=pltpu.HBM)
    dma = pltpu.SemaphoreType.DMA
    conv_out, fgrad, kgrad = pl.pallas_call(
        body,
        out_shape=(
            jax.ShapeDtypeStruct((CL * H, W), F32),
            jax.ShapeDtypeStruct((CL * H, W), F32),
            jax.ShapeDtypeStruct((9 * CL, C), BF16),
        ),
        in_specs=[hbm, vmem, vmem, hbm, hbm],
        out_specs=(hbm,) * 3,
        scratch_shapes=[
            pltpu.VMEM((CL * H, W), BF16),
            pltpu.VMEM((CL * H, W), BF16),
            pltpu.VMEM((9 * CL, C), BF16),
            dma((3,)),
            pltpu.VMEM((CL * H, W), F32),
            pltpu.VMEM((CL, S), F32),
            pltpu.VMEM((CL, S), F32),
            pltpu.VMEM((CL, S), F32),
            pltpu.VMEM((9 * CL, S), BF16),
            pltpu.VMEM((C, 9 * CL), BF16),
            pltpu.VMEM((C, S), BF16),
            pltpu.VMEM((C, W), BF16),
            pltpu.VMEM((2 * CL, W), BF16),
            pltpu.VMEM((2, 2 * CL, W), BF16),
            pltpu.VMEM((2, 1, W), F32),
            pltpu.VMEM((NY, 1, W), F32),
            pltpu.VMEM((NZ, 1, W), F32),
            pltpu.VMEM((2, 1, W), F32),
            pltpu.VMEM((NY, 1, W), F32),
            pltpu.VMEM((NZ, 1, W), F32),
            pltpu.VMEM((C, S), BF16),
            pltpu.VMEM((3, 2 * CL, S), BF16),
            pltpu.VMEM((2, CL, S), BF16),
            pltpu.VMEM((CL, S), BF16),
            pltpu.VMEM((2, 4, 6, CH, W), F32),
            pltpu.VMEM((4, 6, CH, W), BF16),
            pltpu.VMEM((4, 6, CH, W), BF16),
            pltpu.VMEM((NQ, CH, W), BF16),
            pltpu.VMEM((31, CH, W), BF16),
            pltpu.VMEM((2, NQ, CH, W), BF16),
            pltpu.VMEM((9 * CL, S), F32),
            pltpu.VMEM((CL, S), F32),
            pltpu.VMEM((CL * H, W), F32),
            pltpu.VMEM((CL * H, W), F32),
            dma((2,)), dma((2,)),
            dma((7,)), dma((7,)),
            dma((8,)), dma((8,)),
            dma((14,)), dma((14,)),
            dma((14,)), dma((14,)),
            dma((4,)), dma((4,)),
            dma((4,)), dma((4,)),
            dma((31,)), dma((31,)),
            dma((31,)), dma((NQ,)),
            dma((NQ,)), dma((NQ,)),
            dma((2, NQ)),
            dma((2,)),
        ],
        compiler_params=pltpu.CompilerParams(
            collective_id=0, has_side_effects=True, vmem_limit_bytes=62 * 1024 * 1024
        ),
        name="strip",
    )(
        features.reshape(CL * H, W),
        gain.reshape(1, CL),
        bias.reshape(1, CL),
        kernel.reshape(9 * CL, C),
        cotangent.reshape(CL * H, W),
    )
    shape = features.shape
    return (
        conv_out.astype(BF16).reshape(shape),
        fgrad.astype(BF16).reshape(shape),
        (kgrad.astype(F32) * (2.0 ** -8)).reshape(kernel.shape),
    )


def solution(mesh):
    in_specs = (
        P("ch", None, None, "lon"),
        P("ch"),
        P("ch"),
        P(None, None, "ch", None),
        P("ch", None, None, "lon"),
    )
    out_specs = (P("ch", None, None, "lon"), P("ch", None, None, "lon"), P(None, None, "ch", None))
    return jax.shard_map(
        per_device, mesh=mesh, in_specs=in_specs, out_specs=out_specs, check_vma=False
    )
```

```python
import functools

import jax
import jax.numpy as jnp
from jax import lax
from jax.experimental import pallas as pl
from jax.experimental.pallas import tpu as pltpu
from jax.sharding import PartitionSpec as P

C = 512
G = 32
CL = 64
H = 8
W = 128
S = H * W
NZ, NY = 8, 4
NQ = 24
CH = 48
NEAR = sorted(
    ((dz, dy) for dz in range(NZ) for dy in range(NY) if dz or dy),
    key=lambda o: min(o[0], NZ - o[0]) + 2 * min(o[1], NY - o[1]),
)
MESH = pl.DeviceIdType.MESH
F32 = jnp.float32
BF16 = jnp.bfloat16


def body(
    feat_in, gain, bias, w_in, cot_in,
    conv_out, fgrad, kgrad,
    feat, cot, w, in_s, tmp, x2, xh, dact, patch, wt, cotall, halo, edge, edge_in,
    c_st, y_st, z_st, c_t, y_t, z_t,
    convb, convr, convp, convq, convown, g3, gsend, gcore, hb, rsbuf, gfin, zz, agr, conv_f, fg_f,
    edge_s, edge_r, cot_s, cot_r, halo_s, halo_r, st_s, st_r, t_s, t_r,
    conv_s, conv_r, core_s, core_r, rs_s, rs_r, ag_s, ag_r, fw_s, fw_r, kg_s, out_s,
):
    lon = lax.axis_index("lon")
    ch = lax.axis_index("ch")
    z, yc = lon // 8, lon % 8
    yh, core = yc // 2, yc % 2
    x, yl = ch // 2, ch % 2
    n_lon = 64

    def at_lon(d):
        return (lax.rem(lon + d + n_lon, n_lon), ch)

    def at_ch(k):
        return (lon, lax.rem(ch + k, 8))

    def at_x(k):
        return (lon, lax.rem(x + k, 4) * 2 + yl)

    def at_y(k):
        return (z * 8 + lax.rem(yh + k, NY) * 2 + core, ch)

    def at_z(k):
        return (lax.rem(z + k, 8) * 8 + yc, ch)

    partner = (lon + 1 - 2 * core, ch)
    beside = (lon, ch + 1 - 2 * yl)

    def remote(src, dst, ss, rs, dev):
        return pltpu.make_async_remote_copy(
            src_ref=src, dst_ref=dst, send_sem=ss, recv_sem=rs, device_id=dev, device_id_type=MESH
        )

    loads = [
        pltpu.make_async_copy(a, b, in_s.at[i])
        for i, (a, b) in enumerate(((feat_in, feat), (cot_in, cot), (w_in, w)))
    ]
    for cp in loads:
        cp.start()

    barrier = pltpu.get_barrier_semaphore()
    for count, where in ((8, at_ch), (8, at_z), (NY, at_y)):
        for k in range(1, count):
            pl.semaphore_signal(barrier, inc=1, device_id=where(k), device_id_type=MESH)
    for d in (-1, 1):
        pl.semaphore_signal(barrier, inc=1, device_id=at_lon(d), device_id_type=MESH)

    lane = lax.broadcasted_iota(jnp.int32, (CL, W), 1)
    group = lax.broadcasted_iota(jnp.int32, (CL, W), 0) // 16

    my_rows = pl.ds(pl.multiple_of(ch * CL, CL), CL)

    loads[0].wait()
    tmp[...] = feat[...].astype(F32)
    total = jnp.zeros((CL, W), F32)
    total2 = jnp.zeros((CL, W), F32)
    for h in range(H):
        row = tmp[pl.ds(h, CL, stride=H), :]
        x2[:, h * W:(h + 1) * W] = row
        total += row
        total2 += row * row

    def pack(a, b):
        a = jnp.sum(a, axis=1, keepdims=True)
        b = jnp.sum(b, axis=1, keepdims=True)
        both = jnp.where(lane == group, a, 0.0) + jnp.where(lane == group + 4, b, 0.0)
        return jnp.sum(both, axis=0, keepdims=True)

    def unpack(vec):
        full = jnp.broadcast_to(vec, (CL, W))
        a = jnp.sum(jnp.where(lane == group, full, 0.0), axis=1, keepdims=True)
        b = jnp.sum(jnp.where(lane == group + 4, full, 0.0), axis=1, keepdims=True)
        return a, b

    def column(ref):
        r = lax.broadcasted_iota(jnp.int32, (CL, CL), 0)
        c = lax.broadcasted_iota(jnp.int32, (CL, CL), 1)
        return jnp.sum(jnp.where(r == c, jnp.broadcast_to(ref[...], (CL, CL)), 0.0), axis=1, keepdims=True)

    def rounds(bufs, ss, rs):
        def sends(buf, count, base, where):
            return [
                remote(buf.at[0], buf.at[k], ss.at[base + k], rs.at[base + k], where(k))
                for k in range(1, count)
            ]

        return (
            sends(bufs[0], NZ, 0, at_z),
            sends(bufs[1], 2, 8, lambda k: partner),
            sends(bufs[2], NY, 10, at_y),
        )

    def start(copies):
        for cp in copies:
            cp.start()

    def arrive(copies):
        for cp in copies:
            cp.wait_recv()

    def add_up(buf):
        acc = buf[0]
        for k in range(1, buf.shape[0]):
            acc = acc + buf[k]
        return acc

    z_st[0] = pack(total, total2)
    loads[1].wait()
    tmp[...] = cot[...].astype(F32)
    for h in range(H):
        cotall[my_rows, h * W:(h + 1) * W] = tmp[pl.ds(h, CL, stride=H), :].astype(BF16)
    pl.semaphore_wait(barrier, 19)

    st = rounds((z_st, c_st, y_st), st_s, st_r)
    start(st[0])
    its_rows = pl.ds(pl.multiple_of((ch + 1 - 2 * yl) * CL, CL), CL)
    cot_pair = [remote(cotall.at[my_rows], cotall.at[my_rows], cot_s.at[0], cot_r.at[0], beside)]
    cot_mine = [
        remote(cotall.at[my_rows], cotall.at[my_rows], cot_s.at[k], cot_r.at[k], at_x(k))
        for k in (2, 1, 3)
    ]
    cot_its = [
        remote(cotall.at[its_rows], cotall.at[its_rows], cot_s.at[3 + k], cot_r.at[3 + k], at_x(k))
        for k in (1, 3)
    ]
    two_rows = pl.ds(pl.multiple_of((lax.rem(x + 2, 4) * 2 + yl) * CL, CL), CL)
    cot_two = [remote(cotall.at[two_rows], cotall.at[two_rows], cot_s.at[5], cot_r.at[5], beside)]
    start(cot_pair + cot_mine)

    for part, src in ((0, None), (1, x2)):
        e = jnp.zeros((CL, W), F32)
        for h in range(H):
            if src is None:
                row = cotall[my_rows, h * W:(h + 1) * W].astype(F32)
            else:
                row = src[:, h * W:(h + 1) * W]
            e = jnp.where(lane == h, row[:, W - 1:W], e)
            e = jnp.where(lane == H + h, row[:, 0:1], e)
        edge[part * CL:(part + 1) * CL, :] = e.astype(BF16)
    edges = [
        remote(edge, edge_in.at[0], edge_s.at[0], edge_r.at[0], at_lon(1)),
        remote(edge, edge_in.at[1], edge_s.at[1], edge_r.at[1], at_lon(-1)),
    ]
    start(edges)
    loads[2].wait()
    for i in range(4):
        wt[:, i * 128:(i + 1) * 128] = w[i * 128:(i + 1) * 128, :].astype(F32).T.astype(BF16)
    wt[:, 512:576] = w[512:576, :].astype(F32).T.astype(BF16)

    arrive(cot_pair)
    start(cot_its)
    arrive(st[0])
    c_st[0] = add_up(z_st)
    start(st[1])
    arrive(st[1])
    y_st[0] = add_up(c_st)
    start(st[2])
    arrive(cot_mine[:1])
    start(cot_two)

    arrive(edges)
    lane2 = lax.broadcasted_iota(jnp.int32, (2 * CL, W), 1)
    rim = jnp.where(lane2 < H, edge_in[0].astype(F32), edge_in[1].astype(F32))
    halo[my_rows, :] = rim[0:CL].astype(BF16)
    halos = [
        remote(halo.at[my_rows], halo.at[my_rows], halo_s.at[k], halo_r.at[k], at_ch(k))
        for k in range(1, 8)
    ]
    start(halos)

    gain_c = column(gain)
    bias_c = column(bias)
    n = float(16 * H * W * n_lon)
    zero = jnp.zeros((192, W), BF16)
    patch[0:192, 0:W] = zero
    patch[384:576, S - W:S] = zero

    arrive(st[2])
    m1, m2 = unpack(add_up(y_st))
    mean = m1 / n
    var = m2 / n - mean * mean
    rstd = 1.0 / jnp.sqrt(var + 1e-06)

    rim_pre = (rim[CL:2 * CL] - mean) * rstd * gain_c + bias_c
    rim_act = rim_pre * jax.nn.sigmoid(rim_pre)
    for h in range(H):
        cols = slice(h * W, (h + 1) * W)
        norm = (x2[:, cols] - mean) * rstd
        pre = norm * gain_c + bias_c
        sig = jax.nn.sigmoid(pre)
        xh[:, cols] = norm
        dact[:, cols] = sig * (1.0 + pre * (1.0 - sig)) * gain_c
        act = pre * sig
        left = jnp.where(lane == 0, rim_act[:, h:h + 1], pltpu.roll(act, 1, 1))
        right = jnp.where(lane == W - 1, rim_act[:, H + h:H + h + 1], pltpu.roll(act, W - 1, 1))
        for s, v in enumerate((left, act, right)):
            v = v.astype(BF16)
            for r in range(3):
                to = h + 1 - r
                if 0 <= to < H:
                    patch[r * 192 + s * CL:r * 192 + (s + 1) * CL, to * W:(to + 1) * W] = v

    my_j = lax.rem(yh - z + 8, 4)
    my_q = my_j * NZ + z
    owner = my_j < 3

    def to(tz, ty):
        return (tz * 8 + ty * 2 + core, ch)

    def swap(i):
        return remote(gsend.at[i], gcore.at[i], core_s.at[i], core_r.at[i], partner)

    def send_sums(i):
        lc = lax.rem(x + (0, 1, 3, 2)[i], 4)
        swap(i).wait_recv()
        for rc in range(6):
            hb[lc * 6 + rc] = (g3[core, i, rc] + gcore[i, rc].astype(F32)).astype(BF16)
        for rc in range(6):
            q = lc * 6 + rc
            tz = lax.rem(q, NZ)
            ty = lax.rem(q // NZ + tz, NY)
            slot = lax.rem(tz - z + NZ, NZ) * NY + lax.rem(ty - yh + NY, NY)

            @pl.when(q != my_q)
            def _(q=q, tz=tz, ty=ty, slot=slot):
                remote(hb.at[q], rsbuf.at[slot], rs_s.at[0], rs_r.at[slot], to(tz, ty)).start()

    for i in range(4):
        d = (0, 1, 3, 2)[i]
        if d:
            if d != 2:
                remote(
                    cotall.at[my_rows], cotall.at[my_rows], cot_s.at[0], cot_r.at[4 - d], beside
                ).wait_recv()
            remote(cotall.at[my_rows], cotall.at[my_rows], cot_s.at[0], cot_r.at[7 - d], beside).wait_recv()
        rows = pl.ds(pl.multiple_of(lax.rem(x + d, 4) * W, W), W)
        part = lax.dot_general(
            patch[...], cotall[rows, :], (((1,), (1,)), ((), ())), preferred_element_type=F32
        )
        for rc in range(12):
            g3[rc // 6, i, rc % 6] = part[rc * CH:(rc + 1) * CH]
        gsend[i] = g3[1 - core, i].astype(BF16)
        swap(i).start()
        if i:
            send_sums(i - 1)
    send_sums(3)

    def conv_step(i, _):
        cols = pl.ds(pl.multiple_of(i * 256, 256), 256)
        part = jnp.dot(wt[...], patch[:, cols], preferred_element_type=F32)
        zz[0:C, cols] = part
        convb[:, cols] = part.astype(BF16)
        return 0

    lax.fori_loop(0, 4, conv_step, 0)
    for half in range(2):
        convown[half] = zz[pl.ds(pl.multiple_of(x * W + half * CL, CL), CL), :]

    def pair_rows(k):
        return pl.ds(pl.multiple_of(lax.rem(x + k, 4) * W, W), W)

    convs = [
        remote(convb.at[pair_rows(k)], convr.at[k - 1], conv_s.at[k], conv_r.at[k], at_x(k))
        for k in (2, 1, 3)
    ]
    start(convs)

    arrive(halos)

    def z_step(i, _):
        cols = pl.ds(pl.multiple_of(i * 256, 256), 256)
        zz[:, cols] = jnp.dot(w[...], cotall[:, cols], preferred_element_type=F32)
        return 0

    lax.fori_loop(0, 4, z_step, 0)
    zh = jnp.dot(w[...], halo[...], preferred_element_type=F32)

    def zrows(r, s):
        return slice(r * 192 + s * CL, r * 192 + (s + 1) * CL)

    def rim_sum(s):
        up = jnp.where((lane % H) < H - 1, pltpu.roll(zh[zrows(0, s)], W - 1, 1), 0.0)
        down = jnp.where((lane % H) > 0, pltpu.roll(zh[zrows(2, s)], 1, 1), 0.0)
        return up + zh[zrows(1, s)] + down

    rim0, rim2 = rim_sum(0), rim_sum(2)
    t1 = jnp.zeros((CL, W), F32)
    t2 = jnp.zeros((CL, W), F32)
    for h in range(H):
        u = []
        for s in range(3):
            acc = zz[zrows(1, s), h * W:(h + 1) * W]
            if h + 1 < H:
                acc = acc + zz[zrows(0, s), (h + 1) * W:(h + 2) * W]
            if h >= 1:
                acc = acc + zz[zrows(2, s), (h - 1) * W:h * W]
            u.append(acc)
        agrad = u[1]
        agrad = agrad + jnp.where(lane == W - 1, rim0[:, H + h:H + h + 1], pltpu.roll(u[0], W - 1, 1))
        agrad = agrad + jnp.where(lane == 0, rim2[:, h:h + 1], pltpu.roll(u[2], 1, 1))
        cols = slice(h * W, (h + 1) * W)
        ng = agrad * dact[:, cols]
        agr[:, cols] = ng
        t1 += ng
        t2 += ng * xh[:, cols]
    z_t[0] = pack(t1, t2)
    tt = rounds((z_t, c_t, y_t), t_s, t_r)
    start(tt[0])

    def ag_copy(dz, dy):
        q = lax.min(my_j, 2) * NZ + z
        dev = to(lax.rem(z + dz, NZ), lax.rem(yh + dy, NY))
        return remote(gfin.at[core, q], gfin.at[core, q], ag_s.at[0], ag_r.at[q], dev)

    @pl.when(owner)
    def _():
        acc = hb[my_q].astype(F32)
        for dz, dy in NEAR:
            slot = dz * NY + dy
            remote(hb.at[0], rsbuf.at[slot], rs_s.at[0], rs_r.at[slot], partner).wait_recv()
            acc = acc + rsbuf[slot].astype(F32)
        gfin[core, my_q] = acc.astype(BF16)
        for dz, dy in reversed(NEAR):
            ag_copy(dz, dy).start()

    arrive(tt[0])
    c_t[0] = add_up(z_t)
    start(tt[1])
    arrive(tt[1])
    y_t[0] = add_up(c_t)
    start(tt[2])

    arrive(convs)

    def pair_sum(half, h):
        cols = slice(h * W, (h + 1) * W)
        acc = convown[half, :, cols]
        for k in range(3):
            rows = pl.ds(pl.multiple_of(half * CL, CL), CL)
            acc = acc + convr[k, rows, cols].astype(F32)
        return acc

    for h in range(H):
        convp[:, h * W:(h + 1) * W] = pair_sum(1 - yl, h).astype(BF16)
    conv_pair = remote(convp, convq, conv_s.at[0], conv_r.at[0], beside)
    conv_pair.start()

    arrive(tt[2])
    q1, q2 = unpack(add_up(y_t))
    q1 = q1 / n
    q2 = q2 / n
    for h in range(H):
        cols = slice(h * W, (h + 1) * W)
        fg_f[pl.ds(h, CL, stride=H), :] = rstd * (agr[:, cols] - q1 - xh[:, cols] * q2)

    outs = [
        pltpu.make_async_copy(fg_f, fgrad, out_s.at[0]),
        pltpu.make_async_copy(conv_f, conv_out, out_s.at[1]),
    ]
    outs[0].start()

    arrive([conv_pair])
    for h in range(H):
        cols = slice(h * W, (h + 1) * W)
        conv_f[pl.ds(h, CL, stride=H), :] = pair_sum(yl, h) + convq[:, cols].astype(F32)
    outs[1].start()

    for cp in edges + cot_pair + cot_mine + cot_its + cot_two + halos + convs + [conv_pair]:
        cp.wait_send()
    for part in st + tt:
        for cp in part:
            cp.wait_send()
    for i in range(4):
        swap(i).wait_send()

    @pl.when(owner)
    def _():
        few = pl.ds(0, NQ - 1)
        remote(hb.at[few], hb.at[few], rs_s.at[0], rs_r.at[0], partner).wait_send()

    @pl.when(jnp.logical_not(owner))
    def _():
        remote(hb, hb, rs_s.at[0], rs_r.at[0], partner).wait_send()

    def forward(q, half):
        return remote(gfin.at[half, q], gfin.at[half, q], fw_s.at[0], fw_r.at[q], partner)

    def store(q, half):
        rows = pl.ds(pl.multiple_of((half * 6 + lax.rem(q, 6)) * CH, CH), CH)
        cols = pl.ds(pl.multiple_of(q // 6 * W, W), W)
        pltpu.make_async_copy(gfin.at[half, q], kgrad.at[rows, cols], kg_s.at[0]).start()

    def turn(i):
        return lax.rem((x + (0, 1, 3, 2)[i // 6]) * 6 + i % 6, NQ)

    lag = 4
    for i in range(NQ + lag):
        if i < NQ:
            q = turn(i)

            @pl.when(q != my_q)
            def _(q=q):
                remote(gfin.at[core, q], gfin.at[core, q], ag_s.at[0], ag_r.at[q], partner).wait_recv()

            forward(q, core).start()
            store(q, core)
        if i >= lag:
            q = turn(i - lag)
            forward(q, 1 - core).wait_recv()
            store(q, 1 - core)

    @pl.when(owner)
    def _():
        many = rsbuf.at[pl.ds(1, 31)]
        remote(many, many, ag_s.at[0], ag_r.at[0], partner).wait_send()

    remote(gfin.at[core], gfin.at[core], fw_s.at[0], fw_r.at[0], partner).wait_send()
    for cp in outs:
        cp.wait()
    pltpu.make_async_copy(kgrad, kgrad, kg_s.at[0]).wait()


def per_device(features, gain, bias, kernel, cotangent):
    vmem = pl.BlockSpec(memory_space=pltpu.VMEM)
    hbm = pl.BlockSpec(memory_space=pltpu.HBM)
    dma = pltpu.SemaphoreType.DMA
    conv_out, fgrad, kgrad = pl.pallas_call(
        body,
        out_shape=(
            jax.ShapeDtypeStruct((CL * H, W), F32),
            jax.ShapeDtypeStruct((CL * H, W), F32),
            jax.ShapeDtypeStruct((9 * CL, C), BF16),
        ),
        in_specs=[hbm, vmem, vmem, hbm, hbm],
        out_specs=(hbm,) * 3,
        scratch_shapes=[
            pltpu.VMEM((CL * H, W), BF16),
            pltpu.VMEM((CL * H, W), BF16),
            pltpu.VMEM((9 * CL, C), BF16),
            dma((3,)),
            pltpu.VMEM((CL * H, W), F32),
            pltpu.VMEM((CL, S), F32),
            pltpu.VMEM((CL, S), F32),
            pltpu.VMEM((CL, S), F32),
            pltpu.VMEM((9 * CL, S), BF16),
            pltpu.VMEM((C, 9 * CL), BF16),
            pltpu.VMEM((C, S), BF16),
            pltpu.VMEM((C, W), BF16),
            pltpu.VMEM((2 * CL, W), BF16),
            pltpu.VMEM((2, 2 * CL, W), BF16),
            pltpu.VMEM((2, 1, W), F32),
            pltpu.VMEM((NY, 1, W), F32),
            pltpu.VMEM((NZ, 1, W), F32),
            pltpu.VMEM((2, 1, W), F32),
            pltpu.VMEM((NY, 1, W), F32),
            pltpu.VMEM((NZ, 1, W), F32),
            pltpu.VMEM((C, S), BF16),
            pltpu.VMEM((3, 2 * CL, S), BF16),
            pltpu.VMEM((CL, S), BF16),
            pltpu.VMEM((CL, S), BF16),
            pltpu.VMEM((2, CL, S), F32),
            pltpu.VMEM((2, 4, 6, CH, W), F32),
            pltpu.VMEM((4, 6, CH, W), BF16),
            pltpu.VMEM((4, 6, CH, W), BF16),
            pltpu.VMEM((NQ, CH, W), BF16),
            pltpu.VMEM((32, CH, W), BF16),
            pltpu.VMEM((2, NQ, CH, W), BF16),
            pltpu.VMEM((9 * CL, S), F32),
            pltpu.VMEM((CL, S), F32),
            pltpu.VMEM((CL * H, W), F32),
            pltpu.VMEM((CL * H, W), F32),
            dma((2,)), dma((2,)),
            dma((7,)), dma((7,)),
            dma((8,)), dma((8,)),
            dma((14,)), dma((14,)),
            dma((14,)), dma((14,)),
            dma((4,)), dma((4,)),
            dma((4,)), dma((4,)),
            dma((1,)), dma((32,)),
            dma((1,)), dma((NQ,)),
            dma((1,)), dma((NQ,)),
            dma((1,)),
            dma((2,)),
        ],
        compiler_params=pltpu.CompilerParams(
            collective_id=0, has_side_effects=True, vmem_limit_bytes=62 * 1024 * 1024
        ),
        name="strip",
    )(
        features.reshape(CL * H, W),
        gain.reshape(1, CL),
        bias.reshape(1, CL),
        kernel.reshape(9 * CL, C),
        cotangent.reshape(CL * H, W),
    )
    shape = features.shape
    return (
        conv_out.astype(BF16).reshape(shape),
        fgrad.astype(BF16).reshape(shape),
        (kgrad.astype(F32) * (2.0 ** -8)).reshape(kernel.shape),
    )


def solution(mesh):
    in_specs = (
        P("ch", None, None, "lon"),
        P("ch"),
        P("ch"),
        P(None, None, "ch", None),
        P("ch", None, None, "lon"),
    )
    out_specs = (P("ch", None, None, "lon"), P("ch", None, None, "lon"), P(None, None, "ch", None))
    return jax.shard_map(
        per_device, mesh=mesh, in_specs=in_specs, out_specs=out_specs, check_vma=False
    )
```

```python
import functools

import jax
import jax.numpy as jnp
from jax import lax
from jax.experimental import pallas as pl
from jax.experimental.pallas import tpu as pltpu
from jax.sharding import PartitionSpec as P

C = 512
G = 32
CL = 64
H = 8
W = 128
S = H * W
NZ, NY = 8, 4
NQ = 24
CH = 48
NEAR = sorted(
    ((dz, dy) for dz in range(NZ) for dy in range(NY) if dz or dy),
    key=lambda o: min(o[0], NZ - o[0]) + 2 * min(o[1], NY - o[1]),
)
MESH = pl.DeviceIdType.MESH
F32 = jnp.float32
BF16 = jnp.bfloat16


def body(
    feat_in, gain, bias, w_in, cot_in,
    conv_out, fgrad, kgrad,
    feat, cot, w, in_s, tmp, x2, xh, dact, patch, wt, cotall, halo, edge, edge_in,
    c_st, y_st, z_st, c_t, y_t, z_t,
    convb, convr, convp, convq, convown, g3, gsend, gcore, hb, rsbuf, gfin, zz, agr, conv_f, fg_f,
    edge_s, edge_r, cot_s, cot_r, halo_s, halo_r, st_s, st_r, t_s, t_r,
    conv_s, conv_r, core_s, core_r, rs_s, rs_r, ag_s, ag_r, fw_s, fw_r, kg_s, out_s,
):
    lon = lax.axis_index("lon")
    ch = lax.axis_index("ch")
    z, yc = lon // 8, lon % 8
    yh, core = yc // 2, yc % 2
    x, yl = ch // 2, ch % 2
    n_lon = 64

    def at_lon(d):
        return (lax.rem(lon + d + n_lon, n_lon), ch)

    def at_ch(k):
        return (lon, lax.rem(ch + k, 8))

    def at_x(k):
        return (lon, lax.rem(x + k, 4) * 2 + yl)

    def at_y(k):
        return (z * 8 + lax.rem(yh + k, NY) * 2 + core, ch)

    def at_z(k):
        return (lax.rem(z + k, 8) * 8 + yc, ch)

    partner = (lon + 1 - 2 * core, ch)
    beside = (lon, ch + 1 - 2 * yl)

    def remote(src, dst, ss, rs, dev):
        return pltpu.make_async_remote_copy(
            src_ref=src, dst_ref=dst, send_sem=ss, recv_sem=rs, device_id=dev, device_id_type=MESH
        )

    loads = [
        pltpu.make_async_copy(a, b, in_s.at[i])
        for i, (a, b) in enumerate(((feat_in, feat), (cot_in, cot), (w_in, w)))
    ]
    for cp in loads:
        cp.start()

    barrier = pltpu.get_barrier_semaphore()
    for count, where in ((8, at_ch), (8, at_z), (NY, at_y)):
        for k in range(1, count):
            pl.semaphore_signal(barrier, inc=1, device_id=where(k), device_id_type=MESH)
    for d in (-1, 1):
        pl.semaphore_signal(barrier, inc=1, device_id=at_lon(d), device_id_type=MESH)

    lane = lax.broadcasted_iota(jnp.int32, (CL, W), 1)
    group = lax.broadcasted_iota(jnp.int32, (CL, W), 0) // 16

    my_rows = pl.ds(pl.multiple_of(ch * CL, CL), CL)

    loads[0].wait()
    tmp[...] = feat[...].astype(F32)
    total = jnp.zeros((CL, W), F32)
    total2 = jnp.zeros((CL, W), F32)
    for h in range(H):
        row = tmp[pl.ds(h, CL, stride=H), :]
        x2[:, h * W:(h + 1) * W] = row
        total += row
        total2 += row * row

    def pack(a, b):
        a = jnp.sum(a, axis=1, keepdims=True)
        b = jnp.sum(b, axis=1, keepdims=True)
        both = jnp.where(lane == group, a, 0.0) + jnp.where(lane == group + 4, b, 0.0)
        return jnp.sum(both, axis=0, keepdims=True)

    def unpack(vec):
        full = jnp.broadcast_to(vec, (CL, W))
        a = jnp.sum(jnp.where(lane == group, full, 0.0), axis=1, keepdims=True)
        b = jnp.sum(jnp.where(lane == group + 4, full, 0.0), axis=1, keepdims=True)
        return a, b

    def column(ref):
        r = lax.broadcasted_iota(jnp.int32, (CL, CL), 0)
        c = lax.broadcasted_iota(jnp.int32, (CL, CL), 1)
        return jnp.sum(jnp.where(r == c, jnp.broadcast_to(ref[...], (CL, CL)), 0.0), axis=1, keepdims=True)

    def rounds(bufs, ss, rs):
        def sends(buf, count, base, where):
            return [
                remote(buf.at[0], buf.at[k], ss.at[base + k], rs.at[base + k], where(k))
                for k in range(1, count)
            ]

        return (
            sends(bufs[0], NZ, 0, at_z),
            sends(bufs[1], 2, 8, lambda k: partner),
            sends(bufs[2], NY, 10, at_y),
        )

    def start(copies):
        for cp in copies:
            cp.start()

    def arrive(copies):
        for cp in copies:
            cp.wait_recv()

    def add_up(buf):
        acc = buf[0]
        for k in range(1, buf.shape[0]):
            acc = acc + buf[k]
        return acc

    z_st[0] = pack(total, total2)
    loads[1].wait()
    tmp[...] = cot[...].astype(F32)
    for h in range(H):
        cotall[my_rows, h * W:(h + 1) * W] = tmp[pl.ds(h, CL, stride=H), :].astype(BF16)
    pl.semaphore_wait(barrier, 19)

    st = rounds((z_st, c_st, y_st), st_s, st_r)
    start(st[0])
    its_rows = pl.ds(pl.multiple_of((ch + 1 - 2 * yl) * CL, CL), CL)
    cot_pair = [remote(cotall.at[my_rows], cotall.at[my_rows], cot_s.at[0], cot_r.at[0], beside)]
    cot_mine = [
        remote(cotall.at[my_rows], cotall.at[my_rows], cot_s.at[k], cot_r.at[k], at_x(k))
        for k in (2, 1, 3)
    ]
    cot_its = [
        remote(cotall.at[its_rows], cotall.at[its_rows], cot_s.at[3 + k], cot_r.at[3 + k], at_x(k))
        for k in (1, 3)
    ]
    two_rows = pl.ds(pl.multiple_of((lax.rem(x + 2, 4) * 2 + yl) * CL, CL), CL)
    cot_two = [remote(cotall.at[two_rows], cotall.at[two_rows], cot_s.at[5], cot_r.at[5], beside)]
    start(cot_pair + cot_mine)

    for part, src in ((0, None), (1, x2)):
        e = jnp.zeros((CL, W), F32)
        for h in range(H):
            if src is None:
                row = cotall[my_rows, h * W:(h + 1) * W].astype(F32)
            else:
                row = src[:, h * W:(h + 1) * W]
            e = jnp.where(lane == h, row[:, W - 1:W], e)
            e = jnp.where(lane == H + h, row[:, 0:1], e)
        edge[part * CL:(part + 1) * CL, :] = e.astype(BF16)
    edges = [
        remote(edge, edge_in.at[0], edge_s.at[0], edge_r.at[0], at_lon(1)),
        remote(edge, edge_in.at[1], edge_s.at[1], edge_r.at[1], at_lon(-1)),
    ]
    start(edges)
    loads[2].wait()
    for i in range(4):
        wt[:, i * 128:(i + 1) * 128] = w[i * 128:(i + 1) * 128, :].astype(F32).T.astype(BF16)
    wt[:, 512:576] = w[512:576, :].astype(F32).T.astype(BF16)

    arrive(cot_pair)
    start(cot_its)
    arrive(st[0])
    c_st[0] = add_up(z_st)
    start(st[1])
    arrive(st[1])
    y_st[0] = add_up(c_st)
    start(st[2])
    arrive(cot_mine[:1])
    start(cot_two)

    arrive(edges)
    lane2 = lax.broadcasted_iota(jnp.int32, (2 * CL, W), 1)
    rim = jnp.where(lane2 < H, edge_in[0].astype(F32), edge_in[1].astype(F32))
    halo[my_rows, :] = rim[0:CL].astype(BF16)
    halos = [
        remote(halo.at[my_rows], halo.at[my_rows], halo_s.at[k], halo_r.at[k], at_ch(k))
        for k in range(1, 8)
    ]
    start(halos)

    gain_c = column(gain)
    bias_c = column(bias)
    n = float(16 * H * W * n_lon)
    zero = jnp.zeros((192, W), BF16)
    patch[0:192, 0:W] = zero
    patch[384:576, S - W:S] = zero

    arrive(st[2])
    m1, m2 = unpack(add_up(y_st))
    mean = m1 / n
    var = m2 / n - mean * mean
    rstd = 1.0 / jnp.sqrt(var + 1e-06)

    rim_pre = (rim[CL:2 * CL] - mean) * rstd * gain_c + bias_c
    rim_act = rim_pre * jax.nn.sigmoid(rim_pre)
    for h in range(H):
        cols = slice(h * W, (h + 1) * W)
        norm = (x2[:, cols] - mean) * rstd
        pre = norm * gain_c + bias_c
        sig = jax.nn.sigmoid(pre)
        xh[:, cols] = norm
        dact[:, cols] = sig
        x2[:, cols] = pre
        act = pre * sig
        left = jnp.where(lane == 0, rim_act[:, h:h + 1], pltpu.roll(act, 1, 1))
        right = jnp.where(lane == W - 1, rim_act[:, H + h:H + h + 1], pltpu.roll(act, W - 1, 1))
        for s, v in enumerate((left, act, right)):
            v = v.astype(BF16)
            for r in range(3):
                to = h + 1 - r
                if 0 <= to < H:
                    patch[r * 192 + s * CL:r * 192 + (s + 1) * CL, to * W:(to + 1) * W] = v

    my_j = lax.rem(yh - z + 8, 4)
    my_q = my_j * NZ + z
    owner = my_j < 3

    def to(tz, ty):
        return (tz * 8 + ty * 2 + core, ch)

    def swap(i):
        return remote(gsend.at[i], gcore.at[i], core_s.at[i], core_r.at[i], partner)

    def send_sums(i):
        lc = lax.rem(x + (0, 1, 3, 2)[i], 4)
        swap(i).wait_recv()
        for rc in range(6):
            hb[lc * 6 + rc] = (g3[core, i, rc] + gcore[i, rc].astype(F32)).astype(BF16)
        for dz in (4, 3, 5, 2, 6, 1, 7, 0):
            tz = lax.rem(z + dz, NZ)
            rc = lax.rem(tz - lc * 6 + 4 * NZ, NZ)
            q = lc * 6 + lax.min(rc, 5)
            ty = lax.rem(q // NZ + tz, NY)
            slot = dz * NY + lax.rem(ty - yh + NY, NY)

            @pl.when((rc < 6) & (q != my_q))
            def _(q=q, tz=tz, ty=ty, slot=slot):
                remote(hb.at[q], rsbuf.at[slot], rs_s.at[0], rs_r.at[slot], to(tz, ty)).start()

    for i in range(4):
        d = (0, 1, 3, 2)[i]
        if d:
            if d != 2:
                remote(
                    cotall.at[my_rows], cotall.at[my_rows], cot_s.at[0], cot_r.at[4 - d], beside
                ).wait_recv()
            remote(cotall.at[my_rows], cotall.at[my_rows], cot_s.at[0], cot_r.at[7 - d], beside).wait_recv()
        rows = pl.ds(pl.multiple_of(lax.rem(x + d, 4) * W, W), W)
        part = lax.dot_general(
            patch[...], cotall[rows, :], (((1,), (1,)), ((), ())), preferred_element_type=F32
        )
        for rc in range(12):
            g3[rc // 6, i, rc % 6] = part[rc * CH:(rc + 1) * CH]
        gsend[i] = g3[1 - core, i].astype(BF16)
        swap(i).start()
        if i:
            send_sums(i - 1)
    send_sums(3)

    def conv_step(i, _):
        cols = pl.ds(pl.multiple_of(i * 256, 256), 256)
        part = jnp.dot(wt[...], patch[:, cols], preferred_element_type=F32)
        zz[0:C, cols] = part
        convb[:, cols] = part.astype(BF16)
        return 0

    lax.fori_loop(0, 4, conv_step, 0)
    for half in range(2):
        convown[half] = zz[pl.ds(pl.multiple_of(x * W + half * CL, CL), CL), :]

    def pair_rows(k):
        return pl.ds(pl.multiple_of(lax.rem(x + k, 4) * W, W), W)

    convs = [
        remote(convb.at[pair_rows(k)], convr.at[k - 1], conv_s.at[k], conv_r.at[k], at_x(k))
        for k in (2, 1, 3)
    ]
    start(convs)

    arrive(halos)

    def z_step(i, _):
        cols = pl.ds(pl.multiple_of(i * 256, 256), 256)
        zz[:, cols] = jnp.dot(w[...], cotall[:, cols], preferred_element_type=F32)
        return 0

    lax.fori_loop(0, 4, z_step, 0)
    zh = jnp.dot(w[...], halo[...], preferred_element_type=F32)

    def zrows(r, s):
        return slice(r * 192 + s * CL, r * 192 + (s + 1) * CL)

    def rim_sum(s):
        up = jnp.where((lane % H) < H - 1, pltpu.roll(zh[zrows(0, s)], W - 1, 1), 0.0)
        down = jnp.where((lane % H) > 0, pltpu.roll(zh[zrows(2, s)], 1, 1), 0.0)
        return up + zh[zrows(1, s)] + down

    rim0, rim2 = rim_sum(0), rim_sum(2)
    t1 = jnp.zeros((CL, W), F32)
    t2 = jnp.zeros((CL, W), F32)
    for h in range(H):
        u = []
        for s in range(3):
            acc = zz[zrows(1, s), h * W:(h + 1) * W]
            if h + 1 < H:
                acc = acc + zz[zrows(0, s), (h + 1) * W:(h + 2) * W]
            if h >= 1:
                acc = acc + zz[zrows(2, s), (h - 1) * W:h * W]
            u.append(acc)
        agrad = u[1]
        agrad = agrad + jnp.where(lane == W - 1, rim0[:, H + h:H + h + 1], pltpu.roll(u[0], W - 1, 1))
        agrad = agrad + jnp.where(lane == 0, rim2[:, h:h + 1], pltpu.roll(u[2], 1, 1))
        cols = slice(h * W, (h + 1) * W)
        sig = dact[:, cols]
        ng = agrad * sig * (1.0 + x2[:, cols] * (1.0 - sig)) * gain_c
        agr[:, cols] = ng
        t1 += ng
        t2 += ng * xh[:, cols]
    z_t[0] = pack(t1, t2)
    tt = rounds((z_t, c_t, y_t), t_s, t_r)
    start(tt[0])

    def chunk(half, q):
        rows = pl.ds(pl.multiple_of(lax.rem(q, 6) * CH, CH), CH)
        return gfin.at[half, q // 6, rows]

    def ag_copy(dz, dy):
        q = lax.min(my_j, 2) * NZ + z
        dev = to(lax.rem(z + dz, NZ), lax.rem(yh + dy, NY))
        return remote(chunk(core, q), chunk(core, q), ag_s.at[0], ag_r.at[q], dev)

    @pl.when(owner)
    def _():
        acc = hb[my_q].astype(F32)
        for dz, dy in NEAR:
            slot = dz * NY + dy
            remote(hb.at[0], rsbuf.at[slot], rs_s.at[0], rs_r.at[slot], partner).wait_recv()
            acc = acc + rsbuf[slot].astype(F32)
        gfin[core, my_q // 6, pl.ds(pl.multiple_of(lax.rem(my_q, 6) * CH, CH), CH)] = acc.astype(BF16)
        for dz, dy in reversed(NEAR):
            ag_copy(dz, dy).start()

    arrive(tt[0])
    c_t[0] = add_up(z_t)
    start(tt[1])

    arrive(convs)

    def pair_sum(half, h):
        cols = slice(h * W, (h + 1) * W)
        acc = convown[half, :, cols]
        for k in range(3):
            rows = pl.ds(pl.multiple_of(half * CL, CL), CL)
            acc = acc + convr[k, rows, cols].astype(F32)
        return acc

    for h in range(H):
        convp[:, h * W:(h + 1) * W] = pair_sum(1 - yl, h).astype(BF16)
    conv_pair = remote(convp, convq, conv_s.at[0], conv_r.at[0], beside)
    conv_pair.start()
    arrive(tt[1])
    y_t[0] = add_up(c_t)
    start(tt[2])

    for cp in edges + cot_pair + cot_mine + cot_its + cot_two + halos + convs:
        cp.wait_send()
    for part in st + tt[:2]:
        for cp in part:
            cp.wait_send()
    for i in range(4):
        swap(i).wait_send()

    @pl.when(owner)
    def _():
        few = pl.ds(0, NQ - 1)
        remote(hb.at[few], hb.at[few], rs_s.at[0], rs_r.at[0], partner).wait_send()

    @pl.when(jnp.logical_not(owner))
    def _():
        remote(hb, hb, rs_s.at[0], rs_r.at[0], partner).wait_send()

    def forward(i, half):
        lc = lax.rem(x + (0, 1, 3, 2)[i], 4)
        return remote(gfin.at[half, lc], gfin.at[half, lc], fw_s.at[i], fw_r.at[i], partner)

    def store(i, half):
        lc = lax.rem(x + (0, 1, 3, 2)[i], 4)
        rows = pl.ds(pl.multiple_of(half * 6 * CH, 6 * CH), 6 * CH)
        cols = pl.ds(pl.multiple_of(lc * W, W), W)
        return pltpu.make_async_copy(gfin.at[half, lc], kgrad.at[rows, cols], kg_s.at[half, i])

    def relay(i):
        lc = lax.rem(x + (0, 1, 3, 2)[i], 4)
        for rc in range(6):
            q = lc * 6 + rc

            @pl.when(q != my_q)
            def _(q=q):
                remote(chunk(core, q), chunk(core, q), ag_s.at[0], ag_r.at[q], partner).wait_recv()

        forward(i, core).start()
        store(i, core).start()

    def relayed(i):
        forward(i, 1 - core).wait_recv()
        store(i, 1 - core).start()

    relay(0)
    relay(1)
    relay(2)
    arrive(tt[2])
    q1, q2 = unpack(add_up(y_t))
    q1 = q1 / n
    q2 = q2 / n
    for h in range(H):
        cols = slice(h * W, (h + 1) * W)
        fg_f[pl.ds(h, CL, stride=H), :] = rstd * (agr[:, cols] - q1 - xh[:, cols] * q2)

    outs = [
        pltpu.make_async_copy(fg_f, fgrad, out_s.at[0]),
        pltpu.make_async_copy(conv_f, conv_out, out_s.at[1]),
    ]
    outs[0].start()

    arrive([conv_pair])
    for h in range(H):
        cols = slice(h * W, (h + 1) * W)
        conv_f[pl.ds(h, CL, stride=H), :] = pair_sum(yl, h) + convq[:, cols].astype(F32)
    outs[1].start()

    relayed(0)
    relayed(1)
    relayed(2)
    relay(3)

    @pl.when(owner)
    def _():
        many = rsbuf.at[pl.ds(1, 31)]
        remote(many, many, ag_s.at[0], ag_r.at[0], partner).wait_send()

    for cp in tt[2] + [conv_pair]:
        cp.wait_send()
    for i in range(3):
        forward(i, core).wait_send()
    relayed(3)
    forward(3, core).wait_send()
    for cp in outs:
        cp.wait()
    for i in range(4):
        store(i, core).wait()
        store(i, 1 - core).wait()


def finish(conv_in, fg_in, kg_in, conv_out, fg_out, kg_out, conv_a, fg_a, kg_a, conv_b, fg_b, kg_b, sem):
    loads = [
        pltpu.make_async_copy(a, b, sem.at[i])
        for i, (a, b) in enumerate(((conv_in, conv_a), (fg_in, fg_a), (kg_in, kg_a)))
    ]
    stores = [
        pltpu.make_async_copy(a, b, sem.at[3 + i])
        for i, (a, b) in enumerate(((conv_b, conv_out), (fg_b, fg_out), (kg_b, kg_out)))
    ]
    for i in (2, 0, 1):
        loads[i].start()
    loads[2].wait()
    kg_b[...] = kg_a[...].astype(F32) * (2.0 ** -8)
    stores[2].start()
    loads[0].wait()
    conv_b[...] = conv_a[...].astype(BF16)
    stores[0].start()
    loads[1].wait()
    fg_b[...] = fg_a[...].astype(BF16)
    stores[1].start()
    for cp in stores:
        cp.wait()


def per_device(features, gain, bias, kernel, cotangent):
    vmem = pl.BlockSpec(memory_space=pltpu.VMEM)
    hbm = pl.BlockSpec(memory_space=pltpu.HBM)
    dma = pltpu.SemaphoreType.DMA
    conv_out, fgrad, kgrad = pl.pallas_call(
        body,
        out_shape=(
            jax.ShapeDtypeStruct((CL * H, W), F32),
            jax.ShapeDtypeStruct((CL * H, W), F32),
            jax.ShapeDtypeStruct((9 * CL, C), BF16),
        ),
        in_specs=[hbm, vmem, vmem, hbm, hbm],
        out_specs=(hbm,) * 3,
        scratch_shapes=[
            pltpu.VMEM((CL * H, W), BF16),
            pltpu.VMEM((CL * H, W), BF16),
            pltpu.VMEM((9 * CL, C), BF16),
            dma((3,)),
            pltpu.VMEM((CL * H, W), F32),
            pltpu.VMEM((CL, S), F32),
            pltpu.VMEM((CL, S), F32),
            pltpu.VMEM((CL, S), F32),
            pltpu.VMEM((9 * CL, S), BF16),
            pltpu.VMEM((C, 9 * CL), BF16),
            pltpu.VMEM((C, S), BF16),
            pltpu.VMEM((C, W), BF16),
            pltpu.VMEM((2 * CL, W), BF16),
            pltpu.VMEM((2, 2 * CL, W), BF16),
            pltpu.VMEM((2, 1, W), F32),
            pltpu.VMEM((NY, 1, W), F32),
            pltpu.VMEM((NZ, 1, W), F32),
            pltpu.VMEM((2, 1, W), F32),
            pltpu.VMEM((NY, 1, W), F32),
            pltpu.VMEM((NZ, 1, W), F32),
            pltpu.VMEM((C, S), BF16),
            pltpu.VMEM((3, 2 * CL, S), BF16),
            pltpu.VMEM((CL, S), BF16),
            pltpu.VMEM((CL, S), BF16),
            pltpu.VMEM((2, CL, S), F32),
            pltpu.VMEM((2, 4, 6, CH, W), F32),
            pltpu.VMEM((4, 6, CH, W), BF16),
            pltpu.VMEM((4, 6, CH, W), BF16),
            pltpu.VMEM((NQ, CH, W), BF16),
            pltpu.VMEM((32, CH, W), BF16),
            pltpu.VMEM((2, 4, 6 * CH, W), BF16),
            pltpu.VMEM((9 * CL, S), F32),
            pltpu.VMEM((CL, S), F32),
            pltpu.VMEM((CL * H, W), F32),
            pltpu.VMEM((CL * H, W), F32),
            dma((2,)), dma((2,)),
            dma((7,)), dma((7,)),
            dma((8,)), dma((8,)),
            dma((14,)), dma((14,)),
            dma((14,)), dma((14,)),
            dma((4,)), dma((4,)),
            dma((4,)), dma((4,)),
            dma((1,)), dma((32,)),
            dma((1,)), dma((NQ,)),
            dma((4,)), dma((4,)),
            dma((2, 4)),
            dma((2,)),
        ],
        compiler_params=pltpu.CompilerParams(
            collective_id=0, has_side_effects=True, vmem_limit_bytes=62 * 1024 * 1024
        ),
        name="strip",
    )(
        features.reshape(CL * H, W),
        gain.reshape(1, CL),
        bias.reshape(1, CL),
        kernel.reshape(9 * CL, C),
        cotangent.reshape(CL * H, W),
    )
    maps = ((CL * H, W), F32), ((CL * H, W), F32), ((9 * CL, C), BF16)
    ends = ((CL * H, W), BF16), ((CL * H, W), BF16), ((9 * CL, C), F32)
    conv_out, fgrad, kgrad = pl.pallas_call(
        finish,
        out_shape=tuple(jax.ShapeDtypeStruct(*a) for a in ends),
        in_specs=[hbm] * 3,
        out_specs=(hbm,) * 3,
        scratch_shapes=[pltpu.VMEM(*a) for a in maps + ends] + [dma((6,))],
        compiler_params=pltpu.CompilerParams(vmem_limit_bytes=62 * 1024 * 1024),
        name="finish",
    )(conv_out, fgrad, kgrad)
    shape = features.shape
    return (
        conv_out.reshape(shape),
        fgrad.reshape(shape),
        kgrad.reshape(kernel.shape),
    )


def solution(mesh):
    in_specs = (
        P("ch", None, None, "lon"),
        P("ch"),
        P("ch"),
        P(None, None, "ch", None),
        P("ch", None, None, "lon"),
    )
    out_specs = (P("ch", None, None, "lon"), P("ch", None, None, "lon"), P(None, None, "ch", None))
    return jax.shard_map(
        per_device, mesh=mesh, in_specs=in_specs, out_specs=out_specs, check_vma=False
    )
```

```python
import functools

import jax
import jax.numpy as jnp
from jax import lax
from jax.experimental import pallas as pl
from jax.experimental.pallas import tpu as pltpu
from jax.sharding import PartitionSpec as P

C = 512
G = 32
CL = 64
H = 8
W = 128
S = H * W
NZ, NY = 8, 4
NQ = 24
CH = 48
NEAR = sorted(
    ((dz, dy) for dz in range(NZ) for dy in range(NY) if dz or dy),
    key=lambda o: min(o[0], NZ - o[0]) + 2 * min(o[1], NY - o[1]),
)
MESH = pl.DeviceIdType.MESH
F32 = jnp.float32
BF16 = jnp.bfloat16


def body(
    feat_in, gain_in, bias_in, w_in, cot_in,
    conv_out, fgrad, kgrad,
    feat, cot, w, gain, bias, in_s, tmp, x2, xh, dact, patch, wt, cotall, halo, edge, edge_in,
    c_st, y_st, z_st, c_t, y_t, z_t,
    convb, convr, convp, convq, convown, g3, gsend, gcore, hb, rsbuf, gfin, zz, agr, conv_f, fg_f,
    edge_s, edge_r, cot_s, cot_r, halo_s, halo_r, st_s, st_r, t_s, t_r,
    conv_s, conv_r, core_s, core_r, rs_s, rs_r, ag_s, ag_r, fw_s, fw_r, kg_s, out_s,
):
    lon = lax.axis_index("lon")
    ch = lax.axis_index("ch")
    z, yc = lon // 8, lon % 8
    yh, core = yc // 2, yc % 2
    x, yl = ch // 2, ch % 2
    n_lon = 64

    def at_lon(d):
        return (lax.rem(lon + d + n_lon, n_lon), ch)

    def at_ch(k):
        return (lon, lax.rem(ch + k, 8))

    def at_x(k):
        return (lon, lax.rem(x + k, 4) * 2 + yl)

    def at_y(k):
        return (z * 8 + lax.rem(yh + k, NY) * 2 + core, ch)

    def at_z(k):
        return (lax.rem(z + k, 8) * 8 + yc, ch)

    partner = (lon + 1 - 2 * core, ch)
    beside = (lon, ch + 1 - 2 * yl)

    def remote(src, dst, ss, rs, dev):
        return pltpu.make_async_remote_copy(
            src_ref=src, dst_ref=dst, send_sem=ss, recv_sem=rs, device_id=dev, device_id_type=MESH
        )

    loads = [
        pltpu.make_async_copy(a, b, in_s.at[i])
        for i, (a, b) in enumerate((
            (feat_in, feat), (cot_in, cot), (w_in, w), (gain_in, gain), (bias_in, bias)
        ))
    ]
    for cp in loads:
        cp.start()

    barrier = pltpu.get_barrier_semaphore()
    for count, where in ((8, at_ch), (8, at_z), (NY, at_y)):
        for k in range(1, count):
            pl.semaphore_signal(barrier, inc=1, device_id=where(k), device_id_type=MESH)
    for d in (-1, 1):
        pl.semaphore_signal(barrier, inc=1, device_id=at_lon(d), device_id_type=MESH)

    lane = lax.broadcasted_iota(jnp.int32, (CL, W), 1)
    group = lax.broadcasted_iota(jnp.int32, (CL, W), 0) // 16

    my_rows = pl.ds(pl.multiple_of(ch * CL, CL), CL)

    loads[0].wait()
    tmp[...] = feat[...].astype(F32)
    total = jnp.zeros((CL, W), F32)
    total2 = jnp.zeros((CL, W), F32)
    for h in range(H):
        row = tmp[pl.ds(h, CL, stride=H), :]
        x2[:, h * W:(h + 1) * W] = row
        total += row
        total2 += row * row

    def pack(a, b):
        a = jnp.sum(a, axis=1, keepdims=True)
        b = jnp.sum(b, axis=1, keepdims=True)
        both = jnp.where(lane == group, a, 0.0) + jnp.where(lane == group + 4, b, 0.0)
        return jnp.sum(both, axis=0, keepdims=True)

    def unpack(vec):
        full = jnp.broadcast_to(vec, (CL, W))
        a = jnp.sum(jnp.where(lane == group, full, 0.0), axis=1, keepdims=True)
        b = jnp.sum(jnp.where(lane == group + 4, full, 0.0), axis=1, keepdims=True)
        return a, b

    def column(ref):
        r = lax.broadcasted_iota(jnp.int32, (CL, CL), 0)
        c = lax.broadcasted_iota(jnp.int32, (CL, CL), 1)
        return jnp.sum(jnp.where(r == c, jnp.broadcast_to(ref[...], (CL, CL)), 0.0), axis=1, keepdims=True)

    def rounds(bufs, ss, rs):
        def sends(buf, count, base, where):
            return [
                remote(buf.at[0], buf.at[k], ss.at[base + k], rs.at[base + k], where(k))
                for k in range(1, count)
            ]

        return (
            sends(bufs[0], NZ, 0, at_z),
            sends(bufs[1], 2, 8, lambda k: partner),
            sends(bufs[2], NY, 10, at_y),
        )

    def start(copies):
        for cp in copies:
            cp.start()

    def arrive(copies):
        for cp in copies:
            cp.wait_recv()

    def add_up(buf):
        acc = buf[0]
        for k in range(1, buf.shape[0]):
            acc = acc + buf[k]
        return acc

    z_st[0] = pack(total, total2)
    loads[1].wait()
    tmp[...] = cot[...].astype(F32)
    for h in range(H):
        cotall[my_rows, h * W:(h + 1) * W] = tmp[pl.ds(h, CL, stride=H), :].astype(BF16)
    pl.semaphore_wait(barrier, 19)

    st = rounds((z_st, c_st, y_st), st_s, st_r)
    start(st[0])
    its_rows = pl.ds(pl.multiple_of((ch + 1 - 2 * yl) * CL, CL), CL)
    cot_pair = [remote(cotall.at[my_rows], cotall.at[my_rows], cot_s.at[0], cot_r.at[0], beside)]
    cot_mine = [
        remote(cotall.at[my_rows], cotall.at[my_rows], cot_s.at[k], cot_r.at[k], at_x(k))
        for k in (2, 1, 3)
    ]
    cot_its = [
        remote(cotall.at[its_rows], cotall.at[its_rows], cot_s.at[3 + k], cot_r.at[3 + k], at_x(k))
        for k in (1, 3)
    ]
    two_rows = pl.ds(pl.multiple_of((lax.rem(x + 2, 4) * 2 + yl) * CL, CL), CL)
    cot_two = [remote(cotall.at[two_rows], cotall.at[two_rows], cot_s.at[5], cot_r.at[5], beside)]
    start(cot_pair + cot_mine)

    for part, src in ((0, None), (1, x2)):
        e = jnp.zeros((CL, W), F32)
        for h in range(H):
            if src is None:
                row = cotall[my_rows, h * W:(h + 1) * W].astype(F32)
            else:
                row = src[:, h * W:(h + 1) * W]
            e = jnp.where(lane == h, row[:, W - 1:W], e)
            e = jnp.where(lane == H + h, row[:, 0:1], e)
        edge[part * CL:(part + 1) * CL, :] = e.astype(BF16)
    edges = [
        remote(edge, edge_in.at[0], edge_s.at[0], edge_r.at[0], at_lon(1)),
        remote(edge, edge_in.at[1], edge_s.at[1], edge_r.at[1], at_lon(-1)),
    ]
    start(edges)
    loads[2].wait()
    for i in range(4):
        wt[:, i * 128:(i + 1) * 128] = w[i * 128:(i + 1) * 128, :].astype(F32).T.astype(BF16)
    wt[:, 512:576] = w[512:576, :].astype(F32).T.astype(BF16)

    arrive(cot_pair)
    start(cot_its)
    arrive(st[0])
    c_st[0] = add_up(z_st)
    start(st[1])
    arrive(st[1])
    y_st[0] = add_up(c_st)
    start(st[2])
    arrive(cot_mine[:1])
    start(cot_two)

    arrive(edges)
    lane2 = lax.broadcasted_iota(jnp.int32, (2 * CL, W), 1)
    rim = jnp.where(lane2 < H, edge_in[0].astype(F32), edge_in[1].astype(F32))
    halo[my_rows, :] = rim[0:CL].astype(BF16)
    halos = [
        remote(halo.at[my_rows], halo.at[my_rows], halo_s.at[k], halo_r.at[k], at_ch(k))
        for k in range(1, 8)
    ]
    start(halos)

    loads[3].wait()
    loads[4].wait()
    gain_c = column(gain)
    bias_c = column(bias)
    n = float(16 * H * W * n_lon)
    zero = jnp.zeros((192, W), BF16)
    patch[0:192, 0:W] = zero
    patch[384:576, S - W:S] = zero

    arrive(st[2])
    m1, m2 = unpack(add_up(y_st))
    mean = m1 / n
    var = m2 / n - mean * mean
    rstd = 1.0 / jnp.sqrt(var + 1e-06)

    rim_pre = (rim[CL:2 * CL] - mean) * rstd * gain_c + bias_c
    rim_act = rim_pre * jax.nn.sigmoid(rim_pre)
    for h in range(H):
        cols = slice(h * W, (h + 1) * W)
        norm = (x2[:, cols] - mean) * rstd
        pre = norm * gain_c + bias_c
        sig = jax.nn.sigmoid(pre)
        xh[:, cols] = norm
        dact[:, cols] = sig
        x2[:, cols] = pre
        act = pre * sig
        left = jnp.where(lane == 0, rim_act[:, h:h + 1], pltpu.roll(act, 1, 1))
        right = jnp.where(lane == W - 1, rim_act[:, H + h:H + h + 1], pltpu.roll(act, W - 1, 1))
        for s, v in enumerate((left, act, right)):
            v = v.astype(BF16)
            for r in range(3):
                to = h + 1 - r
                if 0 <= to < H:
                    patch[r * 192 + s * CL:r * 192 + (s + 1) * CL, to * W:(to + 1) * W] = v

    my_j = lax.rem(yh - z + 2 * core + 8, 4)
    my_q = my_j * NZ + z
    owner = my_j < 3

    def to(tz, ty):
        return (tz * 8 + ty * 2 + core, ch)

    def swap(i):
        return remote(gsend.at[i], gcore.at[i], core_s.at[i], core_r.at[i], partner)

    def send_sums(i):
        lc = lax.rem(x + (0, 1, 3, 2)[i], 4)
        swap(i).wait_recv()
        for rc in range(6):
            hb[lc * 6 + rc] = (g3[core, i, rc] + gcore[i, rc].astype(F32)).astype(BF16)
        for dz in (4, 3, 5, 2, 6, 1, 7, 0):
            tz = lax.rem(z + dz, NZ)
            rc = lax.rem(tz - lc * 6 + 4 * NZ, NZ)
            q = lc * 6 + lax.min(rc, 5)
            ty = lax.rem(q // NZ + tz + 2 * core, NY)
            slot = dz * NY + lax.rem(ty - yh + NY, NY)

            @pl.when((rc < 6) & (q != my_q))
            def _(q=q, tz=tz, ty=ty, slot=slot):
                remote(hb.at[q], rsbuf.at[slot], rs_s.at[0], rs_r.at[slot], to(tz, ty)).start()

    for i in range(4):
        d = (0, 1, 3, 2)[i]
        if d:
            if d != 2:
                remote(
                    cotall.at[my_rows], cotall.at[my_rows], cot_s.at[0], cot_r.at[4 - d], beside
                ).wait_recv()
            remote(cotall.at[my_rows], cotall.at[my_rows], cot_s.at[0], cot_r.at[7 - d], beside).wait_recv()
        rows = pl.ds(pl.multiple_of(lax.rem(x + d, 4) * W, W), W)
        part = lax.dot_general(
            patch[...], cotall[rows, :], (((1,), (1,)), ((), ())), preferred_element_type=F32
        )
        for rc in range(12):
            g3[rc // 6, i, rc % 6] = part[rc * CH:(rc + 1) * CH]
        gsend[i] = g3[1 - core, i].astype(BF16)
        swap(i).start()
        if i:
            send_sums(i - 1)
    send_sums(3)

    def conv_step(i, _):
        cols = pl.ds(pl.multiple_of(i * 256, 256), 256)
        part = jnp.dot(wt[...], patch[:, cols], preferred_element_type=F32)
        zz[0:C, cols] = part
        convb[:, cols] = part.astype(BF16)
        return 0

    lax.fori_loop(0, 4, conv_step, 0)
    for half in range(2):
        convown[half] = zz[pl.ds(pl.multiple_of(x * W + half * CL, CL), CL), :]

    def pair_rows(k):
        return pl.ds(pl.multiple_of(lax.rem(x + k, 4) * W, W), W)

    convs = [
        remote(convb.at[pair_rows(k)], convr.at[k - 1], conv_s.at[k], conv_r.at[k], at_x(k))
        for k in (2, 1, 3)
    ]
    start(convs)

    arrive(halos)

    def z_step(i, _):
        cols = pl.ds(pl.multiple_of(i * 256, 256), 256)
        zz[:, cols] = jnp.dot(w[...], cotall[:, cols], preferred_element_type=F32)
        return 0

    lax.fori_loop(0, 4, z_step, 0)
    zh = jnp.dot(w[...], halo[...], preferred_element_type=F32)

    def zrows(r, s):
        return slice(r * 192 + s * CL, r * 192 + (s + 1) * CL)

    def rim_sum(s):
        up = jnp.where((lane % H) < H - 1, pltpu.roll(zh[zrows(0, s)], W - 1, 1), 0.0)
        down = jnp.where((lane % H) > 0, pltpu.roll(zh[zrows(2, s)], 1, 1), 0.0)
        return up + zh[zrows(1, s)] + down

    rim0, rim2 = rim_sum(0), rim_sum(2)
    t1 = jnp.zeros((CL, W), F32)
    t2 = jnp.zeros((CL, W), F32)
    for h in range(H):
        u = []
        for s in range(3):
            acc = zz[zrows(1, s), h * W:(h + 1) * W]
            if h + 1 < H:
                acc = acc + zz[zrows(0, s), (h + 1) * W:(h + 2) * W]
            if h >= 1:
                acc = acc + zz[zrows(2, s), (h - 1) * W:h * W]
            u.append(acc)
        agrad = u[1]
        agrad = agrad + jnp.where(lane == W - 1, rim0[:, H + h:H + h + 1], pltpu.roll(u[0], W - 1, 1))
        agrad = agrad + jnp.where(lane == 0, rim2[:, h:h + 1], pltpu.roll(u[2], 1, 1))
        cols = slice(h * W, (h + 1) * W)
        sig = dact[:, cols]
        ng = agrad * sig * (1.0 + x2[:, cols] * (1.0 - sig)) * gain_c
        agr[:, cols] = ng
        t1 += ng
        t2 += ng * xh[:, cols]
    z_t[0] = pack(t1, t2)
    tt = rounds((z_t, c_t, y_t), t_s, t_r)
    start(tt[0])

    def chunk(half, q):
        rows = pl.ds(pl.multiple_of(lax.rem(q, 6) * CH, CH), CH)
        return gfin.at[half, q // 6, rows]

    def ag_copy(dz, dy):
        q = lax.min(my_j, 2) * NZ + z
        dev = to(lax.rem(z + dz, NZ), lax.rem(yh + dy, NY))
        return remote(chunk(core, q), chunk(core, q), ag_s.at[0], ag_r.at[q], dev)

    @pl.when(owner)
    def _():
        acc = hb[my_q].astype(F32)
        for dz, dy in NEAR:
            slot = dz * NY + dy
            remote(hb.at[0], rsbuf.at[slot], rs_s.at[0], rs_r.at[slot], partner).wait_recv()
            acc = acc + rsbuf[slot].astype(F32)
        gfin[core, my_q // 6, pl.ds(pl.multiple_of(lax.rem(my_q, 6) * CH, CH), CH)] = acc.astype(BF16)
        for dz, dy in reversed(NEAR):
            ag_copy(dz, dy).start()

    arrive(tt[0])
    c_t[0] = add_up(z_t)
    start(tt[1])

    arrive(convs)

    def pair_sum(half, h):
        cols = slice(h * W, (h + 1) * W)
        acc = convown[half, :, cols]
        for k in range(3):
            rows = pl.ds(pl.multiple_of(half * CL, CL), CL)
            acc = acc + convr[k, rows, cols].astype(F32)
        return acc

    for h in range(H):
        convp[:, h * W:(h + 1) * W] = pair_sum(1 - yl, h).astype(BF16)
    conv_pair = remote(convp, convq, conv_s.at[0], conv_r.at[0], beside)
    arrive(tt[1])
    y_t[0] = add_up(c_t)
    start(tt[2])

    for cp in edges + cot_pair + cot_mine + cot_its + cot_two + halos + convs:
        cp.wait_send()
    for part in st + tt[:2]:
        for cp in part:
            cp.wait_send()
    for i in range(4):
        swap(i).wait_send()

    @pl.when(owner)
    def _():
        few = pl.ds(0, NQ - 1)
        remote(hb.at[few], hb.at[few], rs_s.at[0], rs_r.at[0], partner).wait_send()

    @pl.when(jnp.logical_not(owner))
    def _():
        remote(hb, hb, rs_s.at[0], rs_r.at[0], partner).wait_send()

    def forward(i, half):
        lc = lax.rem(x + (0, 1, 3, 2)[i], 4)
        return remote(gfin.at[half, lc], gfin.at[half, lc], fw_s.at[i], fw_r.at[i], partner)

    def store(i, half):
        lc = lax.rem(x + (0, 1, 3, 2)[i], 4)
        rows = pl.ds(pl.multiple_of(half * 6 * CH, 6 * CH), 6 * CH)
        cols = pl.ds(pl.multiple_of(lc * W, W), W)
        return pltpu.make_async_copy(gfin.at[half, lc], kgrad.at[rows, cols], kg_s.at[half, i])

    def relay(i):
        lc = lax.rem(x + (0, 1, 3, 2)[i], 4)
        for rc in range(6):
            q = lc * 6 + rc

            @pl.when(q != my_q)
            def _(q=q):
                remote(chunk(core, q), chunk(core, q), ag_s.at[0], ag_r.at[q], partner).wait_recv()

        forward(i, core).start()
        store(i, core).start()

    def relayed(i):
        forward(i, 1 - core).wait_recv()
        store(i, 1 - core).start()

    relay(0)
    conv_pair.start()
    relay(1)
    relay(2)
    arrive(tt[2])
    q1, q2 = unpack(add_up(y_t))
    q1 = q1 / n
    q2 = q2 / n
    for h in range(H):
        cols = slice(h * W, (h + 1) * W)
        fg_f[pl.ds(h, CL, stride=H), :] = rstd * (agr[:, cols] - q1 - xh[:, cols] * q2)

    outs = [
        pltpu.make_async_copy(fg_f, fgrad, out_s.at[0]),
        pltpu.make_async_copy(conv_f, conv_out, out_s.at[1]),
    ]
    outs[0].start()

    relay(3)
    arrive([conv_pair])
    for h in range(H):
        cols = slice(h * W, (h + 1) * W)
        conv_f[pl.ds(h, CL, stride=H), :] = pair_sum(yl, h) + convq[:, cols].astype(F32)
    outs[1].start()

    relayed(0)
    relayed(1)
    relayed(2)

    @pl.when(owner)
    def _():
        many = rsbuf.at[pl.ds(1, 31)]
        remote(many, many, ag_s.at[0], ag_r.at[0], partner).wait_send()

    for cp in tt[2] + [conv_pair]:
        cp.wait_send()
    for i in range(3):
        forward(i, core).wait_send()
    relayed(3)
    forward(3, core).wait_send()
    for cp in outs:
        cp.wait()
    for i in range(4):
        store(i, core).wait()
        store(i, 1 - core).wait()


def finish(conv_in, fg_in, kg_in, conv_out, fg_out, kg_out, conv_a, fg_a, kg_a, conv_b, fg_b, kg_b, sem):
    pieces = [pl.ds(i * 144, 144) for i in range(4)]
    kg_loads = [pltpu.make_async_copy(kg_in.at[p], kg_a.at[p], sem.at[i]) for i, p in enumerate(pieces)]
    kg_stores = [pltpu.make_async_copy(kg_b.at[p], kg_out.at[p], sem.at[4 + i]) for i, p in enumerate(pieces)]
    loads = [
        pltpu.make_async_copy(conv_in, conv_a, sem.at[8]),
        pltpu.make_async_copy(fg_in, fg_a, sem.at[9]),
    ]
    stores = [
        pltpu.make_async_copy(conv_b, conv_out, sem.at[10]),
        pltpu.make_async_copy(fg_b, fg_out, sem.at[11]),
    ]
    for cp in kg_loads + loads:
        cp.start()
    for i, p in enumerate(pieces):
        kg_loads[i].wait()
        kg_b[p, :] = kg_a[p, :].astype(F32) * (2.0 ** -8)
        kg_stores[i].start()
    loads[0].wait()
    conv_b[...] = conv_a[...].astype(BF16)
    stores[0].start()
    loads[1].wait()
    fg_b[...] = fg_a[...].astype(BF16)
    stores[1].start()
    for cp in kg_stores + stores:
        cp.wait()


def per_device(features, gain, bias, kernel, cotangent):
    hbm = pl.BlockSpec(memory_space=pltpu.HBM)
    dma = pltpu.SemaphoreType.DMA
    conv_out, fgrad, kgrad = pl.pallas_call(
        body,
        out_shape=(
            jax.ShapeDtypeStruct((CL * H, W), F32),
            jax.ShapeDtypeStruct((CL * H, W), F32),
            jax.ShapeDtypeStruct((9 * CL, C), BF16),
        ),
        in_specs=[hbm] * 5,
        out_specs=(hbm,) * 3,
        scratch_shapes=[
            pltpu.VMEM((CL * H, W), BF16),
            pltpu.VMEM((CL * H, W), BF16),
            pltpu.VMEM((9 * CL, C), BF16),
            pltpu.VMEM((1, CL), F32),
            pltpu.VMEM((1, CL), F32),
            dma((5,)),
            pltpu.VMEM((CL * H, W), F32),
            pltpu.VMEM((CL, S), F32),
            pltpu.VMEM((CL, S), F32),
            pltpu.VMEM((CL, S), F32),
            pltpu.VMEM((9 * CL, S), BF16),
            pltpu.VMEM((C, 9 * CL), BF16),
            pltpu.VMEM((C, S), BF16),
            pltpu.VMEM((C, W), BF16),
            pltpu.VMEM((2 * CL, W), BF16),
            pltpu.VMEM((2, 2 * CL, W), BF16),
            pltpu.VMEM((2, 1, W), F32),
            pltpu.VMEM((NY, 1, W), F32),
            pltpu.VMEM((NZ, 1, W), F32),
            pltpu.VMEM((2, 1, W), F32),
            pltpu.VMEM((NY, 1, W), F32),
            pltpu.VMEM((NZ, 1, W), F32),
            pltpu.VMEM((C, S), BF16),
            pltpu.VMEM((3, 2 * CL, S), BF16),
            pltpu.VMEM((CL, S), BF16),
            pltpu.VMEM((CL, S), BF16),
            pltpu.VMEM((2, CL, S), F32),
            pltpu.VMEM((2, 4, 6, CH, W), F32),
            pltpu.VMEM((4, 6, CH, W), BF16),
            pltpu.VMEM((4, 6, CH, W), BF16),
            pltpu.VMEM((NQ, CH, W), BF16),
            pltpu.VMEM((32, CH, W), BF16),
            pltpu.VMEM((2, 4, 6 * CH, W), BF16),
            pltpu.VMEM((9 * CL, S), F32),
            pltpu.VMEM((CL, S), F32),
            pltpu.VMEM((CL * H, W), F32),
            pltpu.VMEM((CL * H, W), F32),
            dma((2,)), dma((2,)),
            dma((7,)), dma((7,)),
            dma((8,)), dma((8,)),
            dma((14,)), dma((14,)),
            dma((14,)), dma((14,)),
            dma((4,)), dma((4,)),
            dma((4,)), dma((4,)),
            dma((1,)), dma((32,)),
            dma((1,)), dma((NQ,)),
            dma((4,)), dma((4,)),
            dma((2, 4)),
            dma((2,)),
        ],
        compiler_params=pltpu.CompilerParams(
            collective_id=0, has_side_effects=True, vmem_limit_bytes=62 * 1024 * 1024
        ),
        name="strip",
    )(
        features.reshape(CL * H, W),
        gain.reshape(1, CL),
        bias.reshape(1, CL),
        kernel.reshape(9 * CL, C),
        cotangent.reshape(CL * H, W),
    )
    maps = ((CL * H, W), F32), ((CL * H, W), F32), ((9 * CL, C), BF16)
    ends = ((CL * H, W), BF16), ((CL * H, W), BF16), ((9 * CL, C), F32)
    conv_out, fgrad, kgrad = pl.pallas_call(
        finish,
        out_shape=tuple(jax.ShapeDtypeStruct(*a) for a in ends),
        in_specs=[hbm] * 3,
        out_specs=(hbm,) * 3,
        scratch_shapes=[pltpu.VMEM(*a) for a in maps + ends] + [dma((12,))],
        compiler_params=pltpu.CompilerParams(vmem_limit_bytes=62 * 1024 * 1024),
        name="finish",
    )(conv_out, fgrad, kgrad)
    shape = features.shape
    return (
        conv_out.reshape(shape),
        fgrad.reshape(shape),
        kgrad.reshape(kernel.shape),
    )


def solution(mesh):
    in_specs = (
        P("ch", None, None, "lon"),
        P("ch"),
        P("ch"),
        P(None, None, "ch", None),
        P("ch", None, None, "lon"),
    )
    out_specs = (P("ch", None, None, "lon"), P("ch", None, None, "lon"), P(None, None, "ch", None))
    return jax.shard_map(
        per_device, mesh=mesh, in_specs=in_specs, out_specs=out_specs, check_vma=False
    )
```

```python
import functools

import jax
import jax.numpy as jnp
from jax import lax
from jax.experimental import pallas as pl
from jax.experimental.pallas import tpu as pltpu
from jax.sharding import PartitionSpec as P

C = 512
G = 32
CL = 64
H = 8
W = 128
S = H * W
NZ, NY = 8, 4
NQ = 24
CH = 48
NEAR = sorted(
    ((dz, dy) for dz in range(NZ) for dy in range(NY) if dz or dy),
    key=lambda o: min(o[0], NZ - o[0]) + 2 * min(o[1], NY - o[1]),
)
MESH = pl.DeviceIdType.MESH
F32 = jnp.float32
BF16 = jnp.bfloat16


def body(
    feat_in, gain_in, bias_in, w_in, cot_in,
    conv_out, fgrad, kgrad,
    feat, cot, w, gain, bias, in_s, tmp, x2, xh, dact, patch, wt, cotall, halo, edge, edge_in,
    c_st, y_st, z_st, c_t, y_t, z_t,
    convb, convr, convp, convq, convown, g3, gsend, gcore, hb, rsbuf, gfin, zz, agr, conv_f, fg_f,
    edge_s, edge_r, cot_s, cot_r, halo_s, halo_r, st_s, st_r, t_s, t_r,
    conv_s, conv_r, core_s, core_r, rs_s, rs_r, ag_s, ag_r, fw_s, fw_r, kg_s, out_s,
):
    lon = lax.axis_index("lon")
    ch = lax.axis_index("ch")
    z, yc = lon // 8, lon % 8
    yh, core = yc // 2, yc % 2
    x, yl = ch // 2, ch % 2
    n_lon = 64

    def at_lon(d):
        return (lax.rem(lon + d + n_lon, n_lon), ch)

    def at_ch(k):
        return (lon, lax.rem(ch + k, 8))

    def at_x(k):
        return (lon, lax.rem(x + k, 4) * 2 + yl)

    def at_y(k):
        return (z * 8 + lax.rem(yh + k, NY) * 2 + core, ch)

    def at_z(k):
        return (lax.rem(z + k, 8) * 8 + yc, ch)

    partner = (lon + 1 - 2 * core, ch)
    beside = (lon, ch + 1 - 2 * yl)

    def remote(src, dst, ss, rs, dev):
        return pltpu.make_async_remote_copy(
            src_ref=src, dst_ref=dst, send_sem=ss, recv_sem=rs, device_id=dev, device_id_type=MESH
        )

    loads = [
        pltpu.make_async_copy(a, b, in_s.at[i])
        for i, (a, b) in enumerate((
            (feat_in, feat), (cot_in, cot), (w_in, w), (gain_in, gain), (bias_in, bias)
        ))
    ]
    for cp in loads:
        cp.start()

    barrier = pltpu.get_barrier_semaphore()
    for count, where in ((8, at_ch), (8, at_z), (NY, at_y)):
        for k in range(1, count):
            pl.semaphore_signal(barrier, inc=1, device_id=where(k), device_id_type=MESH)
    for d in (-1, 1):
        pl.semaphore_signal(barrier, inc=1, device_id=at_lon(d), device_id_type=MESH)

    lane = lax.broadcasted_iota(jnp.int32, (CL, W), 1)
    group = lax.broadcasted_iota(jnp.int32, (CL, W), 0) // 16

    my_rows = pl.ds(pl.multiple_of(ch * CL, CL), CL)

    loads[0].wait()
    tmp[...] = feat[...].astype(F32)
    total = jnp.zeros((CL, W), F32)
    total2 = jnp.zeros((CL, W), F32)
    for h in range(H):
        row = tmp[pl.ds(h, CL, stride=H), :]
        x2[:, h * W:(h + 1) * W] = row
        total += row
        total2 += row * row

    def pack(a, b):
        a = jnp.sum(a, axis=1, keepdims=True)
        b = jnp.sum(b, axis=1, keepdims=True)
        both = jnp.where(lane == group, a, 0.0) + jnp.where(lane == group + 4, b, 0.0)
        return jnp.sum(both, axis=0, keepdims=True)

    def unpack(vec):
        full = jnp.broadcast_to(vec, (CL, W))
        a = jnp.sum(jnp.where(lane == group, full, 0.0), axis=1, keepdims=True)
        b = jnp.sum(jnp.where(lane == group + 4, full, 0.0), axis=1, keepdims=True)
        return a, b

    def column(ref):
        r = lax.broadcasted_iota(jnp.int32, (CL, CL), 0)
        c = lax.broadcasted_iota(jnp.int32, (CL, CL), 1)
        return jnp.sum(jnp.where(r == c, jnp.broadcast_to(ref[...], (CL, CL)), 0.0), axis=1, keepdims=True)

    def rounds(bufs, ss, rs):
        def sends(buf, count, base, where):
            return [
                remote(buf.at[0], buf.at[k], ss.at[base + k], rs.at[base + k], where(k))
                for k in range(1, count)
            ]

        return (
            sends(bufs[0], NZ, 0, at_z),
            sends(bufs[1], 2, 8, lambda k: partner),
            sends(bufs[2], NY, 10, at_y),
        )

    def start(copies):
        for cp in copies:
            cp.start()

    def arrive(copies):
        for cp in copies:
            cp.wait_recv()

    def add_up(buf):
        acc = buf[0]
        for k in range(1, buf.shape[0]):
            acc = acc + buf[k]
        return acc

    z_st[0] = pack(total, total2)
    loads[1].wait()
    tmp[...] = cot[...].astype(F32)
    for h in range(H):
        cotall[my_rows, h * W:(h + 1) * W] = tmp[pl.ds(h, CL, stride=H), :].astype(BF16)
    pl.semaphore_wait(barrier, 19)

    st = rounds((z_st, c_st, y_st), st_s, st_r)
    start(st[0])
    its_rows = pl.ds(pl.multiple_of((ch + 1 - 2 * yl) * CL, CL), CL)
    cot_pair = [remote(cotall.at[my_rows], cotall.at[my_rows], cot_s.at[0], cot_r.at[0], beside)]
    cot_mine = [
        remote(cotall.at[my_rows], cotall.at[my_rows], cot_s.at[k], cot_r.at[k], at_x(k))
        for k in (2, 1, 3)
    ]
    cot_its = [
        remote(cotall.at[its_rows], cotall.at[its_rows], cot_s.at[3 + k], cot_r.at[3 + k], at_x(k))
        for k in (1, 3)
    ]
    two_rows = pl.ds(pl.multiple_of((lax.rem(x + 2, 4) * 2 + yl) * CL, CL), CL)
    cot_two = [remote(cotall.at[two_rows], cotall.at[two_rows], cot_s.at[5], cot_r.at[5], beside)]
    start(cot_pair + cot_mine)

    for part, src in ((0, None), (1, x2)):
        e = jnp.zeros((CL, W), F32)
        for h in range(H):
            if src is None:
                row = cotall[my_rows, h * W:(h + 1) * W].astype(F32)
            else:
                row = src[:, h * W:(h + 1) * W]
            e = jnp.where(lane == h, row[:, W - 1:W], e)
            e = jnp.where(lane == H + h, row[:, 0:1], e)
        edge[part * CL:(part + 1) * CL, :] = e.astype(BF16)
    edges = [
        remote(edge, edge_in.at[0], edge_s.at[0], edge_r.at[0], at_lon(1)),
        remote(edge, edge_in.at[1], edge_s.at[1], edge_r.at[1], at_lon(-1)),
    ]
    start(edges)
    loads[2].wait()
    for i in range(4):
        wt[:, i * 128:(i + 1) * 128] = w[i * 128:(i + 1) * 128, :].astype(F32).T.astype(BF16)
    wt[:, 512:576] = w[512:576, :].astype(F32).T.astype(BF16)

    arrive(cot_pair)
    start(cot_its)
    arrive(st[0])
    c_st[0] = add_up(z_st)
    start(st[1])
    arrive(st[1])
    y_st[0] = add_up(c_st)
    start(st[2])
    arrive(cot_mine[:1])
    start(cot_two)

    arrive(edges)
    lane2 = lax.broadcasted_iota(jnp.int32, (2 * CL, W), 1)
    rim = jnp.where(lane2 < H, edge_in[0].astype(F32), edge_in[1].astype(F32))
    halo[my_rows, :] = rim[0:CL].astype(BF16)
    halos = [
        remote(halo.at[my_rows], halo.at[my_rows], halo_s.at[k], halo_r.at[k], at_ch(k))
        for k in range(1, 8)
    ]
    start(halos)

    loads[3].wait()
    loads[4].wait()
    gain_c = column(gain)
    bias_c = column(bias)
    n = float(16 * H * W * n_lon)
    zero = jnp.zeros((192, W), BF16)
    patch[0:192, 0:W] = zero
    patch[384:576, S - W:S] = zero

    arrive(st[2])
    m1, m2 = unpack(add_up(y_st))
    mean = m1 / n
    var = m2 / n - mean * mean
    rstd = 1.0 / jnp.sqrt(var + 1e-06)

    rim_pre = (rim[CL:2 * CL] - mean) * rstd * gain_c + bias_c
    rim_act = rim_pre * jax.nn.sigmoid(rim_pre)
    for h in range(H):
        cols = slice(h * W, (h + 1) * W)
        norm = (x2[:, cols] - mean) * rstd
        pre = norm * gain_c + bias_c
        sig = jax.nn.sigmoid(pre)
        xh[:, cols] = norm
        dact[:, cols] = sig
        x2[:, cols] = pre
        act = pre * sig
        left = jnp.where(lane == 0, rim_act[:, h:h + 1], pltpu.roll(act, 1, 1))
        right = jnp.where(lane == W - 1, rim_act[:, H + h:H + h + 1], pltpu.roll(act, W - 1, 1))
        for s, v in enumerate((left, act, right)):
            v = v.astype(BF16)
            for r in range(3):
                to = h + 1 - r
                if 0 <= to < H:
                    patch[r * 192 + s * CL:r * 192 + (s + 1) * CL, to * W:(to + 1) * W] = v

    my_j = lax.rem(yh - z + 2 * core + 8, 4)
    my_q = my_j * NZ + z
    owner = my_j < 3

    def to(tz, ty):
        return (tz * 8 + ty * 2 + core, ch)

    def swap(i):
        return remote(gsend.at[i], gcore.at[i], core_s.at[i], core_r.at[i], partner)

    def send_sums(i):
        lc = lax.rem(x + (0, 1, 3, 2)[i], 4)
        swap(i).wait_recv()
        for rc in range(6):
            hb[lc * 6 + rc] = (g3[core, i, rc] + gcore[i, rc].astype(F32)).astype(BF16)
        for dz in (4, 3, 5, 2, 6, 1, 7, 0):
            tz = lax.rem(z + dz, NZ)
            rc = lax.rem(tz - lc * 6 + 4 * NZ, NZ)
            q = lc * 6 + lax.min(rc, 5)
            ty = lax.rem(q // NZ + tz + 2 * core, NY)
            slot = dz * NY + lax.rem(ty - yh + NY, NY)

            @pl.when((rc < 6) & (q != my_q))
            def _(q=q, tz=tz, ty=ty, slot=slot):
                remote(hb.at[q], rsbuf.at[slot], rs_s.at[0], rs_r.at[slot], to(tz, ty)).start()

    for i in range(4):
        d = (0, 1, 3, 2)[i]
        if d:
            if d != 2:
                remote(
                    cotall.at[my_rows], cotall.at[my_rows], cot_s.at[0], cot_r.at[4 - d], beside
                ).wait_recv()
            remote(cotall.at[my_rows], cotall.at[my_rows], cot_s.at[0], cot_r.at[7 - d], beside).wait_recv()
        rows = pl.ds(pl.multiple_of(lax.rem(x + d, 4) * W, W), W)
        part = lax.dot_general(
            patch[...], cotall[rows, :], (((1,), (1,)), ((), ())), preferred_element_type=F32
        )
        for rc in range(12):
            g3[rc // 6, i, rc % 6] = part[rc * CH:(rc + 1) * CH]
        gsend[i] = g3[1 - core, i].astype(BF16)
        swap(i).start()
        if i:
            send_sums(i - 1)
    send_sums(3)

    def conv_step(i, _):
        cols = pl.ds(pl.multiple_of(i * 256, 256), 256)
        part = jnp.dot(wt[...], patch[:, cols], preferred_element_type=F32)
        zz[0:C, cols] = part
        convb[:, cols] = part.astype(BF16)
        return 0

    lax.fori_loop(0, 4, conv_step, 0)
    for half in range(2):
        convown[half] = zz[pl.ds(pl.multiple_of(x * W + half * CL, CL), CL), :]

    def pair_rows(k):
        return pl.ds(pl.multiple_of(lax.rem(x + k, 4) * W, W), W)

    convs = [
        remote(convb.at[pair_rows(k)], convr.at[k - 1], conv_s.at[k], conv_r.at[k], at_x(k))
        for k in (2, 1, 3)
    ]
    start(convs)

    arrive(halos)

    def z_step(i, _):
        cols = pl.ds(pl.multiple_of(i * 256, 256), 256)
        zz[:, cols] = jnp.dot(w[...], cotall[:, cols], preferred_element_type=F32)
        return 0

    lax.fori_loop(0, 4, z_step, 0)
    zh = jnp.dot(w[...], halo[...], preferred_element_type=F32)

    def zrows(r, s):
        return slice(r * 192 + s * CL, r * 192 + (s + 1) * CL)

    def rim_sum(s):
        up = jnp.where((lane % H) < H - 1, pltpu.roll(zh[zrows(0, s)], W - 1, 1), 0.0)
        down = jnp.where((lane % H) > 0, pltpu.roll(zh[zrows(2, s)], 1, 1), 0.0)
        return up + zh[zrows(1, s)] + down

    rim0, rim2 = rim_sum(0), rim_sum(2)
    t1 = jnp.zeros((CL, W), F32)
    t2 = jnp.zeros((CL, W), F32)
    for h in range(H):
        u = []
        for s in range(3):
            acc = zz[zrows(1, s), h * W:(h + 1) * W]
            if h + 1 < H:
                acc = acc + zz[zrows(0, s), (h + 1) * W:(h + 2) * W]
            if h >= 1:
                acc = acc + zz[zrows(2, s), (h - 1) * W:h * W]
            u.append(acc)
        agrad = u[1]
        agrad = agrad + jnp.where(lane == W - 1, rim0[:, H + h:H + h + 1], pltpu.roll(u[0], W - 1, 1))
        agrad = agrad + jnp.where(lane == 0, rim2[:, h:h + 1], pltpu.roll(u[2], 1, 1))
        cols = slice(h * W, (h + 1) * W)
        sig = dact[:, cols]
        ng = agrad * sig * (1.0 + x2[:, cols] * (1.0 - sig)) * gain_c
        agr[:, cols] = ng
        t1 += ng
        t2 += ng * xh[:, cols]
    z_t[0] = pack(t1, t2)
    tt = rounds((z_t, c_t, y_t), t_s, t_r)
    start(tt[0])

    def chunk(half, q):
        rows = pl.ds(pl.multiple_of(lax.rem(q, 6) * CH, CH), CH)
        return gfin.at[half, q // 6, rows]

    def ag_copy(dz, dy):
        q = lax.min(my_j, 2) * NZ + z
        dev = to(lax.rem(z + dz, NZ), lax.rem(yh + dy, NY))
        return remote(chunk(core, q), chunk(core, q), ag_s.at[0], ag_r.at[q], dev)

    @pl.when(owner)
    def _():
        acc = hb[my_q].astype(F32)
        for dz, dy in NEAR:
            slot = dz * NY + dy
            remote(hb.at[0], rsbuf.at[slot], rs_s.at[0], rs_r.at[slot], partner).wait_recv()
            acc = acc + rsbuf[slot].astype(F32)
        gfin[core, my_q // 6, pl.ds(pl.multiple_of(lax.rem(my_q, 6) * CH, CH), CH)] = acc.astype(BF16)
        for dz, dy in reversed(NEAR):
            ag_copy(dz, dy).start()

    arrive(tt[0])
    c_t[0] = add_up(z_t)
    start(tt[1])

    arrive(convs)

    def pair_sum(half, h):
        cols = slice(h * W, (h + 1) * W)
        acc = convown[half, :, cols]
        for k in range(3):
            rows = pl.ds(pl.multiple_of(half * CL, CL), CL)
            acc = acc + convr[k, rows, cols].astype(F32)
        return acc

    for h in range(H):
        convp[:, h * W:(h + 1) * W] = pair_sum(1 - yl, h).astype(BF16)
    conv_pair = remote(convp, convq, conv_s.at[0], conv_r.at[0], beside)
    arrive(tt[1])
    y_t[0] = add_up(c_t)
    start(tt[2])

    for cp in edges + cot_pair + cot_mine + cot_its + cot_two + halos + convs:
        cp.wait_send()
    for part in st + tt[:2]:
        for cp in part:
            cp.wait_send()
    for i in range(4):
        swap(i).wait_send()

    @pl.when(owner)
    def _():
        few = pl.ds(0, NQ - 1)
        remote(hb.at[few], hb.at[few], rs_s.at[0], rs_r.at[0], partner).wait_send()

    @pl.when(jnp.logical_not(owner))
    def _():
        remote(hb, hb, rs_s.at[0], rs_r.at[0], partner).wait_send()

    def forward(i, half):
        lc = lax.rem(x + (0, 1, 3, 2)[i], 4)
        return remote(gfin.at[half, lc], gfin.at[half, lc], fw_s.at[i], fw_r.at[i], partner)

    def store(i, half):
        lc = lax.rem(x + (0, 1, 3, 2)[i], 4)
        rows = pl.ds(pl.multiple_of(half * 6 * CH, 6 * CH), 6 * CH)
        cols = pl.ds(pl.multiple_of(lc * W, W), W)
        return pltpu.make_async_copy(gfin.at[half, lc], kgrad.at[rows, cols], kg_s.at[half, i])

    def relay(i):
        lc = lax.rem(x + (0, 1, 3, 2)[i], 4)
        for rc in range(6):
            q = lc * 6 + rc

            @pl.when(q != my_q)
            def _(q=q):
                remote(chunk(core, q), chunk(core, q), ag_s.at[0], ag_r.at[q], partner).wait_recv()

        forward(i, core).start()
        store(i, core).start()

    def relayed(i):
        forward(i, 1 - core).wait_recv()
        store(i, 1 - core).start()

    relay(0)
    conv_pair.start()
    relay(1)
    relay(2)
    relay(3)
    arrive(tt[2])
    q1, q2 = unpack(add_up(y_t))
    q1 = q1 / n
    q2 = q2 / n
    for h in range(H):
        cols = slice(h * W, (h + 1) * W)
        fg_f[pl.ds(h, CL, stride=H), :] = rstd * (agr[:, cols] - q1 - xh[:, cols] * q2)

    outs = [
        pltpu.make_async_copy(fg_f, fgrad, out_s.at[0]),
        pltpu.make_async_copy(conv_f, conv_out, out_s.at[1]),
    ]
    outs[0].start()

    arrive([conv_pair])
    for h in range(H):
        cols = slice(h * W, (h + 1) * W)
        conv_f[pl.ds(h, CL, stride=H), :] = pair_sum(yl, h) + convq[:, cols].astype(F32)
    outs[1].start()

    relayed(0)
    relayed(1)
    relayed(2)

    @pl.when(owner)
    def _():
        many = rsbuf.at[pl.ds(1, 31)]
        remote(many, many, ag_s.at[0], ag_r.at[0], partner).wait_send()

    for cp in tt[2] + [conv_pair]:
        cp.wait_send()
    for i in range(3):
        forward(i, core).wait_send()
    relayed(3)
    forward(3, core).wait_send()
    for cp in outs:
        cp.wait()
    for i in range(4):
        store(i, core).wait()
        store(i, 1 - core).wait()


def finish(conv_in, fg_in, kg_in, conv_out, fg_out, kg_out, conv_a, fg_a, kg_a, conv_b, fg_b, kg_b, sem):
    pieces = [pl.ds(i * 144, 144) for i in range(4)]
    kg_loads = [pltpu.make_async_copy(kg_in.at[p], kg_a.at[p], sem.at[i]) for i, p in enumerate(pieces)]
    kg_stores = [pltpu.make_async_copy(kg_b.at[p], kg_out.at[p], sem.at[4 + i]) for i, p in enumerate(pieces)]
    loads = [
        pltpu.make_async_copy(conv_in, conv_a, sem.at[8]),
        pltpu.make_async_copy(fg_in, fg_a, sem.at[9]),
    ]
    stores = [
        pltpu.make_async_copy(conv_b, conv_out, sem.at[10]),
        pltpu.make_async_copy(fg_b, fg_out, sem.at[11]),
    ]
    for cp in kg_loads + loads:
        cp.start()
    for i, p in enumerate(pieces):
        kg_loads[i].wait()
        kg_b[p, :] = kg_a[p, :].astype(F32) * (2.0 ** -8)
        kg_stores[i].start()
    loads[0].wait()
    conv_b[...] = conv_a[...].astype(BF16)
    stores[0].start()
    loads[1].wait()
    fg_b[...] = fg_a[...].astype(BF16)
    stores[1].start()
    for cp in kg_stores + stores:
        cp.wait()


def per_device(features, gain, bias, kernel, cotangent):
    hbm = pl.BlockSpec(memory_space=pltpu.HBM)
    dma = pltpu.SemaphoreType.DMA
    conv_out, fgrad, kgrad = pl.pallas_call(
        body,
        out_shape=(
            jax.ShapeDtypeStruct((CL * H, W), F32),
            jax.ShapeDtypeStruct((CL * H, W), F32),
            jax.ShapeDtypeStruct((9 * CL, C), BF16),
        ),
        in_specs=[hbm] * 5,
        out_specs=(hbm,) * 3,
        scratch_shapes=[
            pltpu.VMEM((CL * H, W), BF16),
            pltpu.VMEM((CL * H, W), BF16),
            pltpu.VMEM((9 * CL, C), BF16),
            pltpu.VMEM((1, CL), F32),
            pltpu.VMEM((1, CL), F32),
            dma((5,)),
            pltpu.VMEM((CL * H, W), F32),
            pltpu.VMEM((CL, S), F32),
            pltpu.VMEM((CL, S), F32),
            pltpu.VMEM((CL, S), F32),
            pltpu.VMEM((9 * CL, S), BF16),
            pltpu.VMEM((C, 9 * CL), BF16),
            pltpu.VMEM((C, S), BF16),
            pltpu.VMEM((C, W), BF16),
            pltpu.VMEM((2 * CL, W), BF16),
            pltpu.VMEM((2, 2 * CL, W), BF16),
            pltpu.VMEM((2, 1, W), F32),
            pltpu.VMEM((NY, 1, W), F32),
            pltpu.VMEM((NZ, 1, W), F32),
            pltpu.VMEM((2, 1, W), F32),
            pltpu.VMEM((NY, 1, W), F32),
            pltpu.VMEM((NZ, 1, W), F32),
            pltpu.VMEM((C, S), BF16),
            pltpu.VMEM((3, 2 * CL, S), BF16),
            pltpu.VMEM((CL, S), BF16),
            pltpu.VMEM((CL, S), BF16),
            pltpu.VMEM((2, CL, S), F32),
            pltpu.VMEM((2, 4, 6, CH, W), F32),
            pltpu.VMEM((4, 6, CH, W), BF16),
            pltpu.VMEM((4, 6, CH, W), BF16),
            pltpu.VMEM((NQ, CH, W), BF16),
            pltpu.VMEM((32, CH, W), BF16),
            pltpu.VMEM((2, 4, 6 * CH, W), BF16),
            pltpu.VMEM((9 * CL, S), F32),
            pltpu.VMEM((CL, S), F32),
            pltpu.VMEM((CL * H, W), F32),
            pltpu.VMEM((CL * H, W), F32),
            dma((2,)), dma((2,)),
            dma((7,)), dma((7,)),
            dma((8,)), dma((8,)),
            dma((14,)), dma((14,)),
            dma((14,)), dma((14,)),
            dma((4,)), dma((4,)),
            dma((4,)), dma((4,)),
            dma((1,)), dma((32,)),
            dma((1,)), dma((NQ,)),
            dma((4,)), dma((4,)),
            dma((2, 4)),
            dma((2,)),
        ],
        compiler_params=pltpu.CompilerParams(
            collective_id=0, has_side_effects=True, vmem_limit_bytes=62 * 1024 * 1024
        ),
        name="strip",
    )(
        features.reshape(CL * H, W),
        gain.reshape(1, CL),
        bias.reshape(1, CL),
        kernel.reshape(9 * CL, C),
        cotangent.reshape(CL * H, W),
    )
    maps = ((CL * H, W), F32), ((CL * H, W), F32), ((9 * CL, C), BF16)
    ends = ((CL * H, W), BF16), ((CL * H, W), BF16), ((9 * CL, C), F32)
    conv_out, fgrad, kgrad = pl.pallas_call(
        finish,
        out_shape=tuple(jax.ShapeDtypeStruct(*a) for a in ends),
        in_specs=[hbm] * 3,
        out_specs=(hbm,) * 3,
        scratch_shapes=[pltpu.VMEM(*a) for a in maps + ends] + [dma((12,))],
        compiler_params=pltpu.CompilerParams(vmem_limit_bytes=62 * 1024 * 1024),
        name="finish",
    )(conv_out, fgrad, kgrad)
    shape = features.shape
    return (
        conv_out.reshape(shape),
        fgrad.reshape(shape),
        kgrad.reshape(kernel.shape),
    )


def solution(mesh):
    in_specs = (
        P("ch", None, None, "lon"),
        P("ch"),
        P("ch"),
        P(None, None, "ch", None),
        P("ch", None, None, "lon"),
    )
    out_specs = (P("ch", None, None, "lon"), P("ch", None, None, "lon"), P(None, None, "ch", None))
    return jax.shard_map(
        per_device, mesh=mesh, in_specs=in_specs, out_specs=out_specs, check_vma=False
    )
```

```python
import functools

import jax
import jax.numpy as jnp
from jax import lax
from jax.experimental import pallas as pl
from jax.experimental.pallas import tpu as pltpu
from jax.sharding import PartitionSpec as P

C = 512
G = 32
CL = 64
H = 8
W = 128
S = H * W
NZ, NY = 8, 4
NQ = 24
CH = 48
NEAR = sorted(
    ((dz, dy) for dz in range(NZ) for dy in range(NY) if dz or dy),
    key=lambda o: min(o[0], NZ - o[0]) + 2 * min(o[1], NY - o[1]),
)
MESH = pl.DeviceIdType.MESH
F32 = jnp.float32
BF16 = jnp.bfloat16


def body(
    feat_in, gain_in, bias_in, w_in, cot_in,
    conv_out, fgrad, kgrad,
    feat, cot, w, gain, bias, in_s, tmp, x2, xh, dact, patch, wt, cotall, halo, edge, edge_in,
    c_st, y_st, z_st, c_t, y_t, z_t,
    convb, convr, convp, convq, convown, g3, gsend, gcore, hb, rsbuf, gfin, zz, agr, conv_f, fg_f,
    edge_s, edge_r, cot_s, cot_r, halo_s, halo_r, st_s, st_r, t_s, t_r,
    conv_s, conv_r, core_s, core_r, rs_s, rs_r, ag_s, ag_r, fw_s, fw_r, kg_s, out_s,
):
    lon = lax.axis_index("lon")
    ch = lax.axis_index("ch")
    z, yc = lon // 8, lon % 8
    yh, core = yc // 2, yc % 2
    x, yl = ch // 2, ch % 2
    n_lon = 64

    def at_lon(d):
        return (lax.rem(lon + d + n_lon, n_lon), ch)

    def at_ch(k):
        return (lon, lax.rem(ch + k, 8))

    def at_x(k):
        return (lon, lax.rem(x + k, 4) * 2 + yl)

    def at_y(k):
        return (z * 8 + lax.rem(yh + k, NY) * 2 + core, ch)

    def at_z(k):
        return (lax.rem(z + k, 8) * 8 + yc, ch)

    partner = (lon + 1 - 2 * core, ch)
    beside = (lon, ch + 1 - 2 * yl)

    def remote(src, dst, ss, rs, dev):
        return pltpu.make_async_remote_copy(
            src_ref=src, dst_ref=dst, send_sem=ss, recv_sem=rs, device_id=dev, device_id_type=MESH
        )

    loads = [
        pltpu.make_async_copy(a, b, in_s.at[i])
        for i, (a, b) in enumerate((
            (feat_in, feat), (cot_in, cot), (w_in, w), (gain_in, gain), (bias_in, bias)
        ))
    ]
    for cp in loads:
        cp.start()

    barrier = pltpu.get_barrier_semaphore()
    for count, where in ((8, at_ch), (8, at_z), (NY, at_y)):
        for k in range(1, count):
            pl.semaphore_signal(barrier, inc=1, device_id=where(k), device_id_type=MESH)
    for d in (-1, 1):
        pl.semaphore_signal(barrier, inc=1, device_id=at_lon(d), device_id_type=MESH)

    lane = lax.broadcasted_iota(jnp.int32, (CL, W), 1)
    group = lax.broadcasted_iota(jnp.int32, (CL, W), 0) // 16

    my_rows = pl.ds(pl.multiple_of(ch * CL, CL), CL)

    loads[0].wait()
    tmp[...] = feat[...].astype(F32)
    total = jnp.zeros((CL, W), F32)
    total2 = jnp.zeros((CL, W), F32)
    for h in range(H):
        row = tmp[pl.ds(h, CL, stride=H), :]
        x2[:, h * W:(h + 1) * W] = row
        total += row
        total2 += row * row

    def pack(a, b):
        a = jnp.sum(a, axis=1, keepdims=True)
        b = jnp.sum(b, axis=1, keepdims=True)
        both = jnp.where(lane == group, a, 0.0) + jnp.where(lane == group + 4, b, 0.0)
        return jnp.sum(both, axis=0, keepdims=True)

    def unpack(vec):
        full = jnp.broadcast_to(vec, (CL, W))
        a = jnp.sum(jnp.where(lane == group, full, 0.0), axis=1, keepdims=True)
        b = jnp.sum(jnp.where(lane == group + 4, full, 0.0), axis=1, keepdims=True)
        return a, b

    def column(ref):
        r = lax.broadcasted_iota(jnp.int32, (CL, CL), 0)
        c = lax.broadcasted_iota(jnp.int32, (CL, CL), 1)
        return jnp.sum(jnp.where(r == c, jnp.broadcast_to(ref[...], (CL, CL)), 0.0), axis=1, keepdims=True)

    def rounds(bufs, ss, rs):
        def sends(buf, count, base, where):
            return [
                remote(buf.at[0], buf.at[k], ss.at[base + k], rs.at[base + k], where(k))
                for k in range(1, count)
            ]

        return (
            sends(bufs[0], NZ, 0, at_z),
            sends(bufs[1], 2, 8, lambda k: partner),
            sends(bufs[2], NY, 10, at_y),
        )

    def start(copies):
        for cp in copies:
            cp.start()

    def arrive(copies):
        for cp in copies:
            cp.wait_recv()

    def add_up(buf):
        acc = buf[0]
        for k in range(1, buf.shape[0]):
            acc = acc + buf[k]
        return acc

    z_st[0] = pack(total, total2)
    loads[1].wait()
    tmp[...] = cot[...].astype(F32)
    for h in range(H):
        cotall[my_rows, h * W:(h + 1) * W] = tmp[pl.ds(h, CL, stride=H), :].astype(BF16)
    pl.semaphore_wait(barrier, 19)

    st = rounds((z_st, c_st, y_st), st_s, st_r)
    start(st[0])
    its_rows = pl.ds(pl.multiple_of((ch + 1 - 2 * yl) * CL, CL), CL)
    cot_pair = [remote(cotall.at[my_rows], cotall.at[my_rows], cot_s.at[0], cot_r.at[0], beside)]
    cot_mine = [
        remote(cotall.at[my_rows], cotall.at[my_rows], cot_s.at[k], cot_r.at[k], at_x(k))
        for k in (2, 1, 3)
    ]
    cot_its = [
        remote(cotall.at[its_rows], cotall.at[its_rows], cot_s.at[3 + k], cot_r.at[3 + k], at_x(k))
        for k in (1, 3)
    ]
    two_rows = pl.ds(pl.multiple_of((lax.rem(x + 2, 4) * 2 + yl) * CL, CL), CL)
    cot_two = [remote(cotall.at[two_rows], cotall.at[two_rows], cot_s.at[5], cot_r.at[5], beside)]
    start(cot_pair + cot_mine)

    for part, src in ((0, None), (1, x2)):
        e = jnp.zeros((CL, W), F32)
        for h in range(H):
            if src is None:
                row = cotall[my_rows, h * W:(h + 1) * W].astype(F32)
            else:
                row = src[:, h * W:(h + 1) * W]
            e = jnp.where(lane == h, row[:, W - 1:W], e)
            e = jnp.where(lane == H + h, row[:, 0:1], e)
        edge[part * CL:(part + 1) * CL, :] = e.astype(BF16)
    edges = [
        remote(edge, edge_in.at[0], edge_s.at[0], edge_r.at[0], at_lon(1)),
        remote(edge, edge_in.at[1], edge_s.at[1], edge_r.at[1], at_lon(-1)),
    ]
    start(edges)
    arrive(cot_pair)
    start(cot_its)
    arrive(st[0])
    c_st[0] = add_up(z_st)
    start(st[1])
    arrive(st[1])
    y_st[0] = add_up(c_st)
    start(st[2])
    arrive(cot_mine[:1])
    start(cot_two)

    arrive(edges)
    lane2 = lax.broadcasted_iota(jnp.int32, (2 * CL, W), 1)
    rim = jnp.where(lane2 < H, edge_in[0].astype(F32), edge_in[1].astype(F32))
    halo[my_rows, :] = rim[0:CL].astype(BF16)
    halos = [
        remote(halo.at[my_rows], halo.at[my_rows], halo_s.at[k], halo_r.at[k], at_ch(k))
        for k in range(1, 8)
    ]
    start(halos)

    loads[2].wait()
    for i in range(4):
        wt[:, i * 128:(i + 1) * 128] = w[i * 128:(i + 1) * 128, :].astype(F32).T.astype(BF16)
    wt[:, 512:576] = w[512:576, :].astype(F32).T.astype(BF16)

    loads[3].wait()
    loads[4].wait()
    gain_c = column(gain)
    bias_c = column(bias)
    n = float(16 * H * W * n_lon)
    zero = jnp.zeros((192, W), BF16)
    patch[0:192, 0:W] = zero
    patch[384:576, S - W:S] = zero

    arrive(st[2])
    m1, m2 = unpack(add_up(y_st))
    mean = m1 / n
    var = m2 / n - mean * mean
    rstd = 1.0 / jnp.sqrt(var + 1e-06)

    rim_pre = (rim[CL:2 * CL] - mean) * rstd * gain_c + bias_c
    rim_act = rim_pre * jax.nn.sigmoid(rim_pre)
    for h in range(H):
        cols = slice(h * W, (h + 1) * W)
        norm = (x2[:, cols] - mean) * rstd
        pre = norm * gain_c + bias_c
        sig = jax.nn.sigmoid(pre)
        xh[:, cols] = norm
        dact[:, cols] = sig
        x2[:, cols] = pre
        act = pre * sig
        left = jnp.where(lane == 0, rim_act[:, h:h + 1], pltpu.roll(act, 1, 1))
        right = jnp.where(lane == W - 1, rim_act[:, H + h:H + h + 1], pltpu.roll(act, W - 1, 1))
        for s, v in enumerate((left, act, right)):
            v = v.astype(BF16)
            for r in range(3):
                to = h + 1 - r
                if 0 <= to < H:
                    patch[r * 192 + s * CL:r * 192 + (s + 1) * CL, to * W:(to + 1) * W] = v

    my_j = lax.rem(yh - z + 2 * core + 8, 4)
    my_q = my_j * NZ + z
    owner = my_j < 3

    def to(tz, ty):
        return (tz * 8 + ty * 2 + core, ch)

    def swap(i):
        return remote(gsend.at[i], gcore.at[i], core_s.at[i], core_r.at[i], partner)

    def send_sums(i):
        lc = lax.rem(x + (0, 1, 3, 2)[i], 4)
        swap(i).wait_recv()
        for rc in range(6):
            hb[lc * 6 + rc] = (g3[core, i, rc] + gcore[i, rc].astype(F32)).astype(BF16)
        for dz in (4, 3, 5, 2, 6, 1, 7, 0):
            tz = lax.rem(z + dz, NZ)
            rc = lax.rem(tz - lc * 6 + 4 * NZ, NZ)
            q = lc * 6 + lax.min(rc, 5)
            ty = lax.rem(q // NZ + tz + 2 * core, NY)
            slot = dz * NY + lax.rem(ty - yh + NY, NY)

            @pl.when((rc < 6) & (q != my_q))
            def _(q=q, tz=tz, ty=ty, slot=slot):
                remote(hb.at[q], rsbuf.at[slot], rs_s.at[0], rs_r.at[slot], to(tz, ty)).start()

    for i in range(4):
        d = (0, 1, 3, 2)[i]
        if d:
            if d != 2:
                remote(
                    cotall.at[my_rows], cotall.at[my_rows], cot_s.at[0], cot_r.at[4 - d], beside
                ).wait_recv()
            remote(cotall.at[my_rows], cotall.at[my_rows], cot_s.at[0], cot_r.at[7 - d], beside).wait_recv()
        rows = pl.ds(pl.multiple_of(lax.rem(x + d, 4) * W, W), W)
        part = lax.dot_general(
            patch[...], cotall[rows, :], (((1,), (1,)), ((), ())), preferred_element_type=F32
        )
        for rc in range(12):
            g3[rc // 6, i, rc % 6] = part[rc * CH:(rc + 1) * CH]
        gsend[i] = g3[1 - core, i].astype(BF16)
        swap(i).start()
        if i:
            send_sums(i - 1)
    send_sums(3)

    def conv_step(i, _):
        cols = pl.ds(pl.multiple_of(i * 256, 256), 256)
        part = jnp.dot(wt[...], patch[:, cols], preferred_element_type=F32)
        zz[0:C, cols] = part
        convb[:, cols] = part.astype(BF16)
        return 0

    lax.fori_loop(0, 4, conv_step, 0)
    for half in range(2):
        convown[half] = zz[pl.ds(pl.multiple_of(x * W + half * CL, CL), CL), :]

    def pair_rows(k):
        return pl.ds(pl.multiple_of(lax.rem(x + k, 4) * W, W), W)

    convs = [
        remote(convb.at[pair_rows(k)], convr.at[k - 1], conv_s.at[k], conv_r.at[k], at_x(k))
        for k in (2, 1, 3)
    ]
    start(convs)

    arrive(halos)

    def z_step(i, _):
        cols = pl.ds(pl.multiple_of(i * 256, 256), 256)
        zz[:, cols] = jnp.dot(w[...], cotall[:, cols], preferred_element_type=F32)
        return 0

    lax.fori_loop(0, 4, z_step, 0)
    zh = jnp.dot(w[...], halo[...], preferred_element_type=F32)

    def zrows(r, s):
        return slice(r * 192 + s * CL, r * 192 + (s + 1) * CL)

    def rim_sum(s):
        up = jnp.where((lane % H) < H - 1, pltpu.roll(zh[zrows(0, s)], W - 1, 1), 0.0)
        down = jnp.where((lane % H) > 0, pltpu.roll(zh[zrows(2, s)], 1, 1), 0.0)
        return up + zh[zrows(1, s)] + down

    rim0, rim2 = rim_sum(0), rim_sum(2)
    t1 = jnp.zeros((CL, W), F32)
    t2 = jnp.zeros((CL, W), F32)
    for h in range(H):
        u = []
        for s in range(3):
            acc = zz[zrows(1, s), h * W:(h + 1) * W]
            if h + 1 < H:
                acc = acc + zz[zrows(0, s), (h + 1) * W:(h + 2) * W]
            if h >= 1:
                acc = acc + zz[zrows(2, s), (h - 1) * W:h * W]
            u.append(acc)
        agrad = u[1]
        agrad = agrad + jnp.where(lane == W - 1, rim0[:, H + h:H + h + 1], pltpu.roll(u[0], W - 1, 1))
        agrad = agrad + jnp.where(lane == 0, rim2[:, h:h + 1], pltpu.roll(u[2], 1, 1))
        cols = slice(h * W, (h + 1) * W)
        sig = dact[:, cols]
        ng = agrad * sig * (1.0 + x2[:, cols] * (1.0 - sig)) * gain_c
        agr[:, cols] = ng
        t1 += ng
        t2 += ng * xh[:, cols]
    z_t[0] = pack(t1, t2)
    tt = rounds((z_t, c_t, y_t), t_s, t_r)
    start(tt[0])

    def chunk(half, q):
        rows = pl.ds(pl.multiple_of(lax.rem(q, 6) * CH, CH), CH)
        return gfin.at[half, q // 6, rows]

    def ag_copy(dz, dy):
        q = lax.min(my_j, 2) * NZ + z
        dev = to(lax.rem(z + dz, NZ), lax.rem(yh + dy, NY))
        return remote(chunk(core, q), chunk(core, q), ag_s.at[0], ag_r.at[q], dev)

    @pl.when(owner)
    def _():
        acc = hb[my_q].astype(F32)
        for dz, dy in NEAR:
            slot = dz * NY + dy
            remote(hb.at[0], rsbuf.at[slot], rs_s.at[0], rs_r.at[slot], partner).wait_recv()
            acc = acc + rsbuf[slot].astype(F32)
        gfin[core, my_q // 6, pl.ds(pl.multiple_of(lax.rem(my_q, 6) * CH, CH), CH)] = acc.astype(BF16)
        for dz, dy in reversed(NEAR):
            ag_copy(dz, dy).start()

    arrive(tt[0])
    c_t[0] = add_up(z_t)
    start(tt[1])

    arrive(tt[1])
    y_t[0] = add_up(c_t)
    start(tt[2])

    for cp in edges + cot_pair + cot_mine + cot_its + cot_two + halos:
        cp.wait_send()
    for part in st + tt[:2]:
        for cp in part:
            cp.wait_send()
    for i in range(4):
        swap(i).wait_send()

    @pl.when(owner)
    def _():
        few = pl.ds(0, NQ - 1)
        remote(hb.at[few], hb.at[few], rs_s.at[0], rs_r.at[0], partner).wait_send()

    @pl.when(jnp.logical_not(owner))
    def _():
        remote(hb, hb, rs_s.at[0], rs_r.at[0], partner).wait_send()

    def forward(i, half):
        lc = lax.rem(x + (0, 1, 3, 2)[i], 4)
        return remote(gfin.at[half, lc], gfin.at[half, lc], fw_s.at[i], fw_r.at[i], partner)

    def store(i, half):
        lc = lax.rem(x + (0, 1, 3, 2)[i], 4)
        rows = pl.ds(pl.multiple_of(half * 6 * CH, 6 * CH), 6 * CH)
        cols = pl.ds(pl.multiple_of(lc * W, W), W)
        return pltpu.make_async_copy(gfin.at[half, lc], kgrad.at[rows, cols], kg_s.at[half, i])

    def relay(i):
        lc = lax.rem(x + (0, 1, 3, 2)[i], 4)
        for rc in range(6):
            q = lc * 6 + rc

            @pl.when(q != my_q)
            def _(q=q):
                remote(chunk(core, q), chunk(core, q), ag_s.at[0], ag_r.at[q], partner).wait_recv()

        forward(i, core).start()
        store(i, core).start()

    def relayed(i):
        forward(i, 1 - core).wait_recv()
        store(i, 1 - core).start()

    relay(0)
    arrive(convs)

    def pair_sum(half, h):
        cols = slice(h * W, (h + 1) * W)
        acc = convown[half, :, cols]
        for k in range(3):
            rows = pl.ds(pl.multiple_of(half * CL, CL), CL)
            acc = acc + convr[k, rows, cols].astype(F32)
        return acc

    for h in range(H):
        convp[:, h * W:(h + 1) * W] = pair_sum(1 - yl, h).astype(BF16)
    conv_pair = remote(convp, convq, conv_s.at[0], conv_r.at[0], beside)
    conv_pair.start()
    relay(1)
    relay(2)
    relay(3)
    arrive(tt[2])
    q1, q2 = unpack(add_up(y_t))
    q1 = q1 / n
    q2 = q2 / n
    for h in range(H):
        cols = slice(h * W, (h + 1) * W)
        fg_f[pl.ds(h, CL, stride=H), :] = rstd * (agr[:, cols] - q1 - xh[:, cols] * q2)

    outs = [
        pltpu.make_async_copy(fg_f, fgrad, out_s.at[0]),
        pltpu.make_async_copy(conv_f, conv_out, out_s.at[1]),
    ]
    outs[0].start()

    arrive([conv_pair])
    for h in range(H):
        cols = slice(h * W, (h + 1) * W)
        conv_f[pl.ds(h, CL, stride=H), :] = pair_sum(yl, h) + convq[:, cols].astype(F32)
    outs[1].start()

    relayed(0)
    relayed(1)
    relayed(2)

    @pl.when(owner)
    def _():
        many = rsbuf.at[pl.ds(1, 31)]
        remote(many, many, ag_s.at[0], ag_r.at[0], partner).wait_send()

    for cp in tt[2] + convs + [conv_pair]:
        cp.wait_send()
    for i in range(3):
        forward(i, core).wait_send()
    relayed(3)
    forward(3, core).wait_send()
    for cp in outs:
        cp.wait()
    for i in range(4):
        store(i, core).wait()
        store(i, 1 - core).wait()


def finish(conv_in, fg_in, kg_in, conv_out, fg_out, kg_out, conv_a, fg_a, kg_a, conv_b, fg_b, kg_b, sem):
    pieces = [pl.ds(i * 144, 144) for i in range(4)]
    kg_loads = [pltpu.make_async_copy(kg_in.at[p], kg_a.at[p], sem.at[i]) for i, p in enumerate(pieces)]
    kg_stores = [pltpu.make_async_copy(kg_b.at[p], kg_out.at[p], sem.at[4 + i]) for i, p in enumerate(pieces)]
    loads = [
        pltpu.make_async_copy(conv_in, conv_a, sem.at[8]),
        pltpu.make_async_copy(fg_in, fg_a, sem.at[9]),
    ]
    stores = [
        pltpu.make_async_copy(conv_b, conv_out, sem.at[10]),
        pltpu.make_async_copy(fg_b, fg_out, sem.at[11]),
    ]
    for cp in kg_loads + loads:
        cp.start()
    for i, p in enumerate(pieces):
        kg_loads[i].wait()
        kg_b[p, :] = kg_a[p, :].astype(F32) * (2.0 ** -8)
        kg_stores[i].start()
    loads[0].wait()
    conv_b[...] = conv_a[...].astype(BF16)
    stores[0].start()
    loads[1].wait()
    fg_b[...] = fg_a[...].astype(BF16)
    stores[1].start()
    for cp in kg_stores + stores:
        cp.wait()


def per_device(features, gain, bias, kernel, cotangent):
    hbm = pl.BlockSpec(memory_space=pltpu.HBM)
    dma = pltpu.SemaphoreType.DMA
    conv_out, fgrad, kgrad = pl.pallas_call(
        body,
        out_shape=(
            jax.ShapeDtypeStruct((CL * H, W), F32),
            jax.ShapeDtypeStruct((CL * H, W), F32),
            jax.ShapeDtypeStruct((9 * CL, C), BF16),
        ),
        in_specs=[hbm] * 5,
        out_specs=(hbm,) * 3,
        scratch_shapes=[
            pltpu.VMEM((CL * H, W), BF16),
            pltpu.VMEM((CL * H, W), BF16),
            pltpu.VMEM((9 * CL, C), BF16),
            pltpu.VMEM((1, CL), F32),
            pltpu.VMEM((1, CL), F32),
            dma((5,)),
            pltpu.VMEM((CL * H, W), F32),
            pltpu.VMEM((CL, S), F32),
            pltpu.VMEM((CL, S), F32),
            pltpu.VMEM((CL, S), F32),
            pltpu.VMEM((9 * CL, S), BF16),
            pltpu.VMEM((C, 9 * CL), BF16),
            pltpu.VMEM((C, S), BF16),
            pltpu.VMEM((C, W), BF16),
            pltpu.VMEM((2 * CL, W), BF16),
            pltpu.VMEM((2, 2 * CL, W), BF16),
            pltpu.VMEM((2, 1, W), F32),
            pltpu.VMEM((NY, 1, W), F32),
            pltpu.VMEM((NZ, 1, W), F32),
            pltpu.VMEM((2, 1, W), F32),
            pltpu.VMEM((NY, 1, W), F32),
            pltpu.VMEM((NZ, 1, W), F32),
            pltpu.VMEM((C, S), BF16),
            pltpu.VMEM((3, 2 * CL, S), BF16),
            pltpu.VMEM((CL, S), BF16),
            pltpu.VMEM((CL, S), BF16),
            pltpu.VMEM((2, CL, S), F32),
            pltpu.VMEM((2, 4, 6, CH, W), F32),
            pltpu.VMEM((4, 6, CH, W), BF16),
            pltpu.VMEM((4, 6, CH, W), BF16),
            pltpu.VMEM((NQ, CH, W), BF16),
            pltpu.VMEM((32, CH, W), BF16),
            pltpu.VMEM((2, 4, 6 * CH, W), BF16),
            pltpu.VMEM((9 * CL, S), F32),
            pltpu.VMEM((CL, S), F32),
            pltpu.VMEM((CL * H, W), F32),
            pltpu.VMEM((CL * H, W), F32),
            dma((2,)), dma((2,)),
            dma((7,)), dma((7,)),
            dma((8,)), dma((8,)),
            dma((14,)), dma((14,)),
            dma((14,)), dma((14,)),
            dma((4,)), dma((4,)),
            dma((4,)), dma((4,)),
            dma((1,)), dma((32,)),
            dma((1,)), dma((NQ,)),
            dma((4,)), dma((4,)),
            dma((2, 4)),
            dma((2,)),
        ],
        compiler_params=pltpu.CompilerParams(
            collective_id=0, has_side_effects=True, vmem_limit_bytes=62 * 1024 * 1024
        ),
        name="strip",
    )(
        features.reshape(CL * H, W),
        gain.reshape(1, CL),
        bias.reshape(1, CL),
        kernel.reshape(9 * CL, C),
        cotangent.reshape(CL * H, W),
    )
    maps = ((CL * H, W), F32), ((CL * H, W), F32), ((9 * CL, C), BF16)
    ends = ((CL * H, W), BF16), ((CL * H, W), BF16), ((9 * CL, C), F32)
    conv_out, fgrad, kgrad = pl.pallas_call(
        finish,
        out_shape=tuple(jax.ShapeDtypeStruct(*a) for a in ends),
        in_specs=[hbm] * 3,
        out_specs=(hbm,) * 3,
        scratch_shapes=[pltpu.VMEM(*a) for a in maps + ends] + [dma((12,))],
        compiler_params=pltpu.CompilerParams(vmem_limit_bytes=62 * 1024 * 1024),
        name="finish",
    )(conv_out, fgrad, kgrad)
    shape = features.shape
    return (
        conv_out.reshape(shape),
        fgrad.reshape(shape),
        kgrad.reshape(kernel.shape),
    )


def solution(mesh):
    in_specs = (
        P("ch", None, None, "lon"),
        P("ch"),
        P("ch"),
        P(None, None, "ch", None),
        P("ch", None, None, "lon"),
    )
    out_specs = (P("ch", None, None, "lon"), P("ch", None, None, "lon"), P(None, None, "ch", None))
    return jax.shard_map(
        per_device, mesh=mesh, in_specs=in_specs, out_specs=out_specs, check_vma=False
    )
```
